32 devices in a mesh: gx: 4 (over x, core), gy: 8 (over z, y).
Axes of the slice: x: 2, y: 2, z: 4, core: 2. Of those that a mesh axis runs over, the one named last changes fastest.
Arguments:
- volume: bfloat16 [32, 64, 2, 256], P('gx', 'gy'), may hold values from -6 to 6
- first_weight: bfloat16 [6912, 256], replicated, may hold values from -0.078125 to 0.078125
- second_weight: bfloat16 [6912, 256], replicated, may hold values from -0.078125 to 0.078125
- cotangent: bfloat16 [32, 64, 2, 256], P('gx', 'gy'), may hold values from -6 to 6
Outputs:
- output: bfloat16 [32, 64, 2, 256], P('gx', 'gy')
- volume_grad: bfloat16 [32, 64, 2, 256], P('gx', 'gy')
- second_grad: float32 [1769472], P(('gx', 'gy'))
The draws below stay inside these ranges and needn't reach their ends.
All inputs are finite; a program needn't handle non-finite values.
Results may differ from the reference program's by a relative error of at most 0.015.
Values may be sent and summed in bfloat16 or wider, within the bound.
No kernel may reach another device: no remote copies, remote signals or barrier semaphores. Data moves between devices by JAX's collectives and lax.ppermute only.
A program may use at most 64 MiB of HBM per device.

```python
import jax
import jax.numpy as jnp
from jax import lax

C = 256
KTAPS = 27
SLAB = 2
NX = 32
NY = 64


def block_levels(stream_key, shape, pieces, low, largest):
    def one(axis_at, shards_of):
        steps = jax.random.uniform(jax.random.fold_in(jax.random.fold_in(stream_key, 6), axis_at), (shards_of,), jnp.float32, low / len(pieces), largest / len(pieces))
        return jnp.repeat(jnp.exp(steps), shape[axis_at] // shards_of).reshape((-1,) + (1,) * (len(shape) - axis_at - 1))

    factor_of = one(*pieces[0])
    for cut in pieces[1:]:
        factor_of = factor_of * one(*cut)
    return factor_of


def bell_draw(key, shape, spread, limit, split=(), held_as=jnp.bfloat16):
    loudness = block_levels(key, shape, split, -0.22, 0.18) if split else 1.0
    values = jax.random.normal(key, shape, jnp.float32) * spread * loudness
    return jnp.minimum(jnp.maximum(values, -limit), limit).astype(held_as)


def setup_inputs(seed: int = 0) -> dict:
    keys = jax.random.split(jax.random.key(seed), 5)
    return {
        "volume": bell_draw(keys[0], (NX, NY, SLAB, C), 1.0, 6.0, ((0, 4), (1, 8))),
        "first_weight": bell_draw(keys[1], (KTAPS * C, C), (KTAPS * C) ** -0.5, 0.078125),
        "second_weight": bell_draw(keys[2], (KTAPS * C, C), (KTAPS * C) ** -0.5, 0.078125),
        "cotangent": bell_draw(keys[3], (NX, NY, SLAB, C), 1.0, 6.0, ((0, 4), (1, 8))),
    }


def pad_field(field):
    wrapped = jnp.pad(field, ((1, 1), (1, 1), (0, 0), (0, 0)), mode='wrap')
    return jnp.pad(wrapped, ((0, 0), (0, 0), (1, 1), (0, 0)))

def correlate(field, kernel):
    padded = pad_field(field.astype(jnp.float32))
    chans = field.shape[3]
    weights = kernel.astype(jnp.float32).reshape(3, 3, 3, chans, kernel.shape[1])
    result = lax.conv_general_dilated(padded[None], weights, (1, 1, 1), 'VALID', dimension_numbers=('NDHWC', 'DHWIO', 'NDHWC'), precision=lax.Precision.HIGHEST)
    return result[0]

def weight_grad(source, grad):
    padded = pad_field(source.astype(jnp.float32))
    gfull = grad.astype(jnp.float32)
    sx, sy, sz = (grad.shape[0], grad.shape[1], grad.shape[2])
    blocks = []
    for a in range(3):
        for b in range(3):
            for e in range(3):
                piece = padded[a:a + sx, b:b + sy, e:e + sz, :]
                blocks.append(jnp.einsum('xyzc,xyzd->cd', piece, gfull, precision=lax.Precision.HIGHEST))
    scale = 1.0 / jnp.sqrt(jnp.float32(NX * NY * SLAB))
    return (jnp.concatenate(blocks, axis=0) * scale).reshape(-1)

def flipped(kernel):
    chans = kernel.shape[1]
    weights = kernel.reshape(3, 3, 3, chans, chans)[::-1, ::-1, ::-1]
    return jnp.transpose(weights, (0, 1, 2, 4, 3)).reshape(KTAPS * chans, chans)

def reference(volume, first_weight, second_weight, cotangent):
    pre = correlate(volume, first_weight)
    hidden = jax.nn.silu(pre).astype(jnp.bfloat16)
    output = correlate(hidden, second_weight).astype(jnp.bfloat16)
    second_grad = weight_grad(hidden, cotangent)
    back = correlate(cotangent, flipped(second_weight))
    sig = jax.nn.sigmoid(pre)
    through = (back * sig * (1.0 + pre * (1.0 - sig))).astype(jnp.bfloat16)
    volume_grad = correlate(through, flipped(first_weight)).astype(jnp.bfloat16)
    return (output, volume_grad, second_grad)
```

```python
import functools

import jax
import jax.numpy as jnp
from jax import lax
from jax.experimental import pallas as pl
from jax.experimental.pallas import tpu as pltpu
from jax.sharding import PartitionSpec as P

AX = ("gx", "gy")
F32 = jnp.float32
BF16 = jnp.bfloat16
CH = 256
ROWS = 27 * CH


def permutation(n_gx, n_gy, move):
    pairs = []
    for i in range(n_gx):
        for j in range(n_gy):
            x, c, z, y = move(i // 2, i % 2, j // 2, j % 2)
            x, z = x % (n_gx // 2), z % (n_gy // 2)
            pairs.append((i * n_gy + j, (x * 2 + c) * n_gy + z * 2 + y))
    return pairs


def dot(a, b):
    return lax.dot_general(a, b, (((1,), (0,)), ((), ())), preferred_element_type=F32)


def dot_t(a, b):
    return lax.dot_general(a, b, (((1,), (1,)), ((), ())), preferred_element_type=F32)


def shifted(v, by):
    if by == 0:
        return v
    axis, n = v.ndim - 2, v.shape[-2]
    if by > 0:
        parts = [lax.slice_in_dim(v, by, n, axis=axis), lax.slice_in_dim(v, 0, by, axis=axis)]
    else:
        parts = [lax.slice_in_dim(v, n + by, n, axis=axis), lax.slice_in_dim(v, 0, n + by, axis=axis)]
    return jnp.concatenate(parts, axis=axis)


def window(v, core):
    n = v.shape[-2]
    first = jnp.concatenate([v[..., n - 4 :, :], v[..., :12, :]], axis=-2)
    return jnp.where(core == 0, first, v[..., 4:20, :])


def gradient_kernel(n_x, n_z, n_taps, strip, block, scale, *refs):
    same, other = refs[: 2 * n_x], refs[2 * n_x : 4 * n_x]
    w_hbm = refs[4 * n_x]
    pre_out, cot_out, own_out = refs[4 * n_x + 1 : 4 * n_x + 4]
    sends = refs[4 * n_x + 4 : 4 * n_x + 3 + n_z]
    w_ref, vol, cot, acc0, acc1, hid, grad, sems = refs[4 * n_x + 3 + n_z :]
    gx, gy = lax.axis_index("gx"), lax.axis_index("gy")
    core, side, z = lax.rem(gx, 2), lax.rem(gy, 2), lax.div(gy, 2)
    full = 16 * n_x

    def weight(k):
        rows = pl.ds(k * 768, 768)
        return pltpu.make_async_copy(w_hbm.at[rows], w_ref.at[rows], sems.at[k])

    for k in range(9):
        weight(k).start()

    for dy in range(2):
        at = side if dy == 0 else 1 - side
        for which in range(2):
            for pair in range(5):
                rows = pl.ds(which * 80 + pair * 16, 16)
                parts = []
                for dx in range(n_x):
                    a = same[dx * 2 + dy][rows, :].astype(F32).reshape(2, 8, 512)
                    b = other[dx * 2 + dy][rows, :].astype(F32).reshape(2, 8, 512)
                    parts += [jnp.where(core == 0, a, b), jnp.where(core == 0, b, a)]
                line = jnp.concatenate(parts, axis=1)
                row = 2 + 8 * at + 2 * pair if pair < 4 else 18 * at
                for s in range(3):
                    if which == 0:
                        vol[s, pl.ds(row, 2)] = shifted(line, s - 1).astype(BF16)
                    else:
                        turned = shifted(line, 1 - s).astype(BF16)
                        cot[s, 0, pl.ds(row, 2)] = turned[..., :CH]
                        cot[s, 1, pl.ds(row, 2)] = turned[..., CH:]
    cot[:, 2] = jnp.zeros_like(cot[:, 2])

    acc0[...] = jnp.zeros_like(acc0)
    acc1[...] = jnp.zeros_like(acc1)

    def tap(k, carry):
        weight(k).wait()
        left = vol[lax.div(k, 3), pl.ds(lax.rem(k, 3), 18)].reshape(18 * full, 512)
        base = pl.multiple_of(k * 768, 256)
        acc0[...] += dot(left, w_ref[pl.ds(base + 256, 512), :])
        acc1[...] += dot(left, w_ref[pl.ds(base, 512), :])
        return carry

    lax.fori_loop(0, 9, tap, 0)

    for half, acc in enumerate((acc0, acc1)):
        pre = acc[pl.ds(full, 16 * full), :]
        hid[:, half * 16 * full : (half + 1) * 16 * full] = (pre * jax.nn.sigmoid(pre)).T.astype(BF16)

    first = lax.div(gx * strip, CH)

    def piece(k, carry):
        t = jnp.minimum(first + k, 26)
        a, b, e = lax.div(t, 9), lax.rem(lax.div(t, 3), 3), lax.rem(t, 3)
        z0 = jnp.where(e == 1, 0, jnp.where(e == 0, 1, 2))
        z1 = jnp.where(e == 1, 1, jnp.where(e == 0, 2, 0))
        rows = pl.ds(3 - b, 16)
        total = dot(hid[:, : 16 * full], cot[a, z0, rows].reshape(16 * full, CH))
        total += dot(hid[:, 16 * full :], cot[a, z1, rows].reshape(16 * full, CH))
        grad[pl.ds(pl.multiple_of(k * CH, CH), CH), :] = total * scale
        return carry

    lax.fori_loop(0, n_taps, piece, 0)

    for k in range(n_z):
        start = gx * strip + (2 * lax.rem(z + k, n_z) + side) * block - first * CH
        if block % 8 == 0:
            value = grad[pl.ds(pl.multiple_of(start, 8), block), :]
        else:
            over = lax.rem(start, 8)
            rows = (block + 7 + 7) // 8 * 8
            value = grad[pl.ds(pl.multiple_of(start - over, 8), rows), :]
            value = pltpu.roll(value, lax.rem(rows - over, rows), 0)[:block]
        if k == 0:
            own_out[...] = value
        else:
            sends[k - 1][...] = value.astype(BF16)

    for half, acc in enumerate((acc0, acc1)):
        rows = acc[pl.ds(pl.multiple_of(side * 8 * full, full), 10 * full), :].reshape(10, full, CH)
        pre_out[:, :, half * CH : (half + 1) * CH] = window(rows, core)
        rows = cot[1, half, pl.ds(side * 8, 12)].astype(F32)
        cot_out[:, :, half * CH : (half + 1) * CH] = window(rows, core).astype(BF16)


def local_kernel(pre_ref, cot_ref, w1_hbm, w2_hbm, out_ref, vgrad_ref, w1, w2, hid, cot, thr, acc, sems):
    def weight(which, k):
        rows = pl.ds(k * 768, 768)
        src, dst = ((w1_hbm, w1), (w2_hbm, w2))[which]
        return pltpu.make_async_copy(src.at[rows], dst.at[rows], sems.at[which, k])

    for which in (1, 0):
        for k in range(9):
            weight(which, k).start()

    pre = pre_ref[...]
    sig = jax.nn.sigmoid(pre)
    for s in range(3):
        hid[s] = shifted(pre * sig, s - 1).astype(BF16)
        cot[s] = shifted(cot_ref[...].astype(F32), s - 1).astype(BF16)

    def back(k, carry):
        left = cot[lax.div(k, 3), pl.ds(lax.rem(k, 3), 10)].reshape(160, 512)
        base = pl.multiple_of((8 - k) * 768, 256)
        w = w2[pl.ds(base, 768), :]
        acc[:, :CH] += dot_t(left[:, :CH], w[256:512]) + dot_t(left[:, CH:], w[:256])
        acc[:, CH:] += dot_t(left[:, :CH], w[512:]) + dot_t(left[:, CH:], w[256:512])
        return carry

    def forward(k, carry):
        left = hid[lax.div(k, 3), pl.ds(lax.rem(k, 3), 8)].reshape(128, 512)
        base = pl.multiple_of(k * 768, 256)
        acc[:128, :CH] += dot(left, w2[pl.ds(base + 256, 512), :])
        acc[:128, CH:] += dot(left, w2[pl.ds(base, 512), :])
        return carry

    def last(k, carry):
        left = thr[lax.div(k, 3), pl.ds(lax.rem(k, 3), 8)].reshape(128, 512)
        base = pl.multiple_of((8 - k) * 768, 256)
        w = w1[pl.ds(base, 768), :]
        acc[:128, :CH] += dot_t(left[:, :CH], w[256:512]) + dot_t(left[:, CH:], w[:256])
        acc[:128, CH:] += dot_t(left[:, :CH], w[512:]) + dot_t(left[:, CH:], w[256:512])
        return carry

    for k in range(9):
        weight(1, k).wait()
    acc[...] = jnp.zeros_like(acc)
    lax.fori_loop(0, 9, back, 0)
    through = acc[...].reshape(10, 16, 512) * sig * (1.0 + pre * (1.0 - sig))
    for s in range(3):
        thr[s] = shifted(through, s - 1).astype(BF16)

    acc[...] = jnp.zeros_like(acc)
    lax.fori_loop(0, 9, forward, 0)
    out_ref[...] = acc[:128].reshape(8, 16, 512)[:, 4:12].astype(BF16)

    for k in range(9):
        weight(0, k).wait()
    acc[...] = jnp.zeros_like(acc)
    lax.fori_loop(0, 9, last, 0)
    vgrad_ref[...] = acc[:128].reshape(8, 16, 512)[:, 4:12].astype(BF16)


def body(volume, first_weight, second_weight, cotangent):
    sx, sy, sz, chans = volume.shape
    n_gx, n_gy = lax.axis_size("gx"), lax.axis_size("gy")
    n_x, n_z = n_gx // 2, n_gy // 2
    scale = 1.0 / float(sx * n_gx * sy * n_gy * sz) ** 0.5
    strip = ROWS // n_gx
    block = strip // n_gy
    n_taps = max(-(-(i + 1) * strip // CH) - i * strip // CH for i in range(n_gx))
    full = sx * n_gx
    side = lax.rem(lax.axis_index("gy"), 2)
    perm = functools.partial(permutation, n_gx, n_gy)

    def lines(v):
        return jnp.transpose(v, (1, 0, 2, 3)).reshape(sy, sx, sz * chans)

    own = jnp.stack([lines(volume), lines(cotangent)])
    edge = lax.dynamic_slice_in_dim(own, side * (sy - 2), 2, axis=1)
    edge = lax.ppermute(edge, AX, perm(lambda x, c, z, y: (x, c, z - 1 + 2 * y, 1 - y)))
    own = jnp.concatenate([own, edge], axis=1).reshape(2 * (sy + 2) * sx, sz * chans)

    same = []
    for dx in range(n_x):
        for dy in range(2):
            if dx == 0 and dy == 0:
                same.append(own)
            else:
                same.append(lax.ppermute(own, AX, perm(lambda x, c, z, y, dx=dx, dy=dy: (x - dx, c, z, y ^ dy))))
    other = [lax.ppermute(v, AX, perm(lambda x, c, z, y: (x, 1 - c, z, y))) for v in same]

    vmem = pl.BlockSpec(memory_space=pltpu.VMEM)
    hbm = pl.BlockSpec(memory_space=pl.ANY)
    results = pl.pallas_call(
        functools.partial(gradient_kernel, n_x, n_z, n_taps, strip, block, scale),
        out_shape=[
            jax.ShapeDtypeStruct((10, 16, 512), F32),
            jax.ShapeDtypeStruct((12, 16, 512), BF16),
            jax.ShapeDtypeStruct((block, CH), F32),
        ]
        + [jax.ShapeDtypeStruct((block, CH), BF16)] * (n_z - 1),
        in_specs=[vmem] * (4 * n_x) + [hbm],
        out_specs=[vmem] * (2 + n_z),
        scratch_shapes=[
            pltpu.VMEM((ROWS, CH), BF16),
            pltpu.VMEM((3, 20, full, 512), BF16),
            pltpu.VMEM((3, 3, 20, full, CH), BF16),
            pltpu.VMEM((18 * full, CH), F32),
            pltpu.VMEM((18 * full, CH), F32),
            pltpu.VMEM((CH, 32 * full), BF16),
            pltpu.VMEM((n_taps * CH + (0 if block % 8 == 0 else 16), CH), F32),
            pltpu.SemaphoreType.DMA((9,)),
        ],
        compiler_params=pltpu.CompilerParams(vmem_limit_bytes=48 * 1024 * 1024),
        cost_estimate=pl.CostEstimate(flops=4 * 10**9, bytes_accessed=6 * 10**6, transcendentals=0),
        name="group_gradient",
    )(*same, *other, first_weight)
    pre, cot, mine, sends = results[0], results[1], results[2], results[3:]

    received = [
        lax.ppermute(v, AX, perm(lambda x, c, z, y, k=k: (x, c, z + k + 1, y))) for k, v in enumerate(sends)
    ]

    output, volume_grad = pl.pallas_call(
        local_kernel,
        out_shape=[jax.ShapeDtypeStruct((sy, sx, 512), BF16)] * 2,
        in_specs=[vmem, vmem, hbm, hbm],
        out_specs=[vmem, vmem],
        scratch_shapes=[
            pltpu.VMEM((ROWS, CH), BF16),
            pltpu.VMEM((ROWS, CH), BF16),
            pltpu.VMEM((3, 10, 16, 512), BF16),
            pltpu.VMEM((3, 12, 16, 512), BF16),
            pltpu.VMEM((3, 10, 16, 512), BF16),
            pltpu.VMEM((160, 512), F32),
            pltpu.SemaphoreType.DMA((2, 9)),
        ],
        compiler_params=pltpu.CompilerParams(vmem_limit_bytes=32 * 1024 * 1024),
        cost_estimate=pl.CostEstimate(flops=4 * 10**9, bytes_accessed=8 * 10**6, transcendentals=0),
        name="local_convolutions",
    )(pre, cot, first_weight, second_weight)

    def cells(v):
        return jnp.transpose(v.reshape(sy, sx, sz, chans), (1, 0, 2, 3))

    total = mine
    for v in received:
        total = total + v.astype(F32)
    return cells(output), cells(volume_grad), total.reshape(-1)


def solution(mesh):
    in_specs = (P("gx", "gy", None, None), P(), P(), P("gx", "gy", None, None))
    out_specs = (P("gx", "gy", None, None), P("gx", "gy", None, None), P(("gx", "gy")))
    return jax.shard_map(body, mesh=mesh, in_specs=in_specs, out_specs=out_specs, check_vma=False)
```

```python
import functools

import jax
import jax.numpy as jnp
from jax import lax
from jax.experimental import pallas as pl
from jax.experimental.pallas import tpu as pltpu
from jax.sharding import PartitionSpec as P

AX = ("gx", "gy")
F32 = jnp.float32
BF16 = jnp.bfloat16
CH = 256
ROWS = 27 * CH


def permutation(n_gx, n_gy, move):
    pairs = []
    for i in range(n_gx):
        for j in range(n_gy):
            x, c, z, y = move(i // 2, i % 2, j // 2, j % 2)
            x, z = x % (n_gx // 2), z % (n_gy // 2)
            pairs.append((i * n_gy + j, (x * 2 + c) * n_gy + z * 2 + y))
    return pairs


def dot(a, b):
    return lax.dot_general(a, b, (((1,), (0,)), ((), ())), preferred_element_type=F32)


def dot_t(a, b):
    return lax.dot_general(a, b, (((1,), (1,)), ((), ())), preferred_element_type=F32)


def shifted(v, by):
    if by == 0:
        return v
    axis, n = v.ndim - 2, v.shape[-2]
    if by > 0:
        parts = [lax.slice_in_dim(v, by, n, axis=axis), lax.slice_in_dim(v, 0, by, axis=axis)]
    else:
        parts = [lax.slice_in_dim(v, n + by, n, axis=axis), lax.slice_in_dim(v, 0, n + by, axis=axis)]
    return jnp.concatenate(parts, axis=axis)


def window(v, core):
    n = v.shape[-2]
    first = jnp.concatenate([v[..., n - 4 :, :], v[..., :12, :]], axis=-2)
    return jnp.where(core == 0, first, v[..., 4:20, :])


def assemble(same, other, core, side, put):
    n_x = len(same) // 2
    for dy in range(2):
        at = side if dy == 0 else 1 - side
        for pair in range(5):
            rows = slice(pair * 16, pair * 16 + 16)
            parts = []
            for dx in range(n_x):
                a = same[dx * 2 + dy][rows, :].astype(F32).reshape(2, 8, 512)
                b = other[dx * 2 + dy][rows, :].astype(F32).reshape(2, 8, 512)
                parts += [jnp.where(core == 0, a, b), jnp.where(core == 0, b, a)]
            put(2 + 8 * at + 2 * pair if pair < 4 else 18 * at, jnp.concatenate(parts, axis=1))


def both(w):
    return jnp.concatenate([w[CH:], w[: 2 * CH]], axis=1)


def place():
    gx, gy = lax.axis_index("gx"), lax.axis_index("gy")
    return gx, lax.rem(gx, 2), lax.div(gy, 2), lax.rem(gy, 2)


def hidden_kernel(n_x, *refs):
    same, other = refs[: 2 * n_x], refs[2 * n_x : 4 * n_x]
    w_ref, pre, hid, vol = refs[4 * n_x :]
    _, core, _, side = place()
    full = 16 * n_x

    def put(row, line):
        for s in range(3):
            vol[s, pl.ds(row, 2)] = shifted(line, s - 1).astype(BF16)

    assemble(same, other, core, side, put)
    for k in range(9):
        left = vol[k // 3, k % 3 : k % 3 + 18].reshape(18 * full, 512)
        term = dot(left, both(w_ref[k * 768 : k * 768 + 768, :]))
        pre[...] = term if k == 0 else pre[...] + term
    inner = pre[full : 17 * full, :]
    hid[...] = (inner * jax.nn.sigmoid(inner)).T.astype(BF16)


def gradient_kernel(n_x, n_z, groups, strip, block, scale, *refs):
    same, other = refs[: 2 * n_x], refs[2 * n_x : 4 * n_x]
    hid, cot, own_out = refs[4 * n_x : 4 * n_x + 3]
    sends = refs[4 * n_x + 3 : 4 * n_x + 2 + n_z]
    grad = refs[-1]
    gx, core, z, side = place()
    full = 16 * n_x

    def put(row, line):
        for s in range(3):
            cot[s, pl.ds(row, 2)] = shifted(line, 1 - s).astype(BF16)

    assemble(same, other, core, side, put)
    first = lax.div(gx * strip, 3 * CH)
    for k in range(groups):
        ab = jnp.minimum(first + k, 8)
        right = cot[lax.div(ab, 3), pl.ds(3 - lax.rem(ab, 3), 16)].reshape(16 * full, 512)
        product = dot(hid[...], right) * scale
        at = k * 3 * CH
        grad[at : at + CH, :] = product[:CH, CH:]
        grad[at + CH : at + 2 * CH, :] = product[:CH, :CH] + product[CH:, CH:]
        grad[at + 2 * CH : at + 3 * CH, :] = product[CH:, :CH]

    for k in range(n_z):
        start = gx * strip + (2 * lax.rem(z + k, n_z) + side) * block - first * 3 * CH
        if block % 8 == 0:
            value = grad[pl.ds(pl.multiple_of(start, 8), block), :]
        else:
            over = lax.rem(start, 8)
            rows = (block + 7 + 7) // 8 * 8
            value = grad[pl.ds(pl.multiple_of(start - over, 8), rows), :]
            value = pltpu.roll(value, lax.rem(rows - over, rows), 0)[:block]
        if k == 0:
            own_out[...] = value
        else:
            sends[k - 1][...] = value.astype(BF16)


def local_kernel(pre_ref, cot_ref, w1, w2, out_ref, vgrad_ref, hid, cot, thr, acc):
    _, core, _, side = place()
    full = cot_ref.shape[2]
    pre = pre_ref[pl.ds(pl.multiple_of(side * 8 * full, full), 10 * full), :]
    pre = window(pre.reshape(10, full, 512), core)
    sig = jax.nn.sigmoid(pre)
    turned = window(cot_ref[1, pl.ds(side * 8, 12)].astype(F32), core)
    for s in range(3):
        hid[s] = shifted(pre * sig, s - 1).astype(BF16)
        cot[s] = shifted(turned, s - 1).astype(BF16)

    for k in range(9):
        left = cot[k // 3, k % 3 : k % 3 + 10].reshape(160, 512)
        term = dot_t(left, both(w2[(8 - k) * 768 : (8 - k) * 768 + 768, :]))
        acc[...] = term if k == 0 else acc[...] + term
    through = acc[...].reshape(10, 16, 512) * sig * (1.0 + pre * (1.0 - sig))
    for s in range(3):
        thr[s] = shifted(through, s - 1).astype(BF16)

    for k in range(9):
        left = hid[k // 3, k % 3 : k % 3 + 8].reshape(128, 512)
        term = dot(left, both(w2[k * 768 : k * 768 + 768, :]))
        acc[:128] = term if k == 0 else acc[:128] + term
    out_ref[...] = acc[:128].reshape(8, 16, 512)[:, 4:12].astype(BF16)

    for k in range(9):
        left = thr[k // 3, k % 3 : k % 3 + 8].reshape(128, 512)
        term = dot_t(left, both(w1[(8 - k) * 768 : (8 - k) * 768 + 768, :]))
        acc[:128] = term if k == 0 else acc[:128] + term
    vgrad_ref[...] = acc[:128].reshape(8, 16, 512)[:, 4:12].astype(BF16)


def extend_kernel(vol, cot, edge, vol_out, cot_out):
    for k, (ref, out) in enumerate(((vol, vol_out), (cot, cot_out))):
        out[:64, :] = ref[...]
        out[64:, :] = edge[k * 16 : k * 16 + 16, :]


def params(mib):
    return pltpu.CompilerParams(vmem_limit_bytes=mib * 1024 * 1024)


def cost(us):
    return pl.CostEstimate(flops=us * 10**9, bytes_accessed=us * 3 * 10**6, transcendentals=0)


def body(volume, first_weight, second_weight, cotangent):
    sx, sy, sz, chans = volume.shape
    n_gx, n_gy = lax.axis_size("gx"), lax.axis_size("gy")
    n_x, n_z = n_gx // 2, n_gy // 2
    scale = 1.0 / float(sx * n_gx * sy * n_gy * sz) ** 0.5
    strip = ROWS // n_gx
    block = strip // n_gy
    groups = max(-(-(i + 1) * strip // (3 * CH)) - i * strip // (3 * CH) for i in range(n_gx))
    full = sx * n_gx
    side = lax.rem(lax.axis_index("gy"), 2)
    perm = functools.partial(permutation, n_gx, n_gy)
    vmem = pl.BlockSpec(memory_space=pltpu.VMEM)

    def lines(v):
        return jnp.transpose(v, (1, 0, 2, 3)).reshape(-1, sz * chans)

    def ends(v):
        return lines(lax.dynamic_slice_in_dim(v, side * (sy - 2), 2, axis=1))

    edge = jnp.concatenate([ends(volume), ends(cotangent)])
    edge = lax.ppermute(edge, AX, perm(lambda x, c, z, y: (x, c, z - 1 + 2 * y, 1 - y)))
    pieces = pl.pallas_call(
        extend_kernel,
        out_shape=[jax.ShapeDtypeStruct((80, 512), BF16)] * 2,
        in_specs=[vmem] * 3,
        out_specs=[vmem] * 2,
        compiler_params=params(4),
        cost_estimate=cost(4),
        name="extend",
    )(lines(volume), lines(cotangent), edge)

    gathered = []
    for piece in pieces:
        same = []
        for dx in range(n_x):
            for dy in range(2):
                if dx == 0 and dy == 0:
                    same.append(piece)
                else:
                    same.append(lax.ppermute(piece, AX, perm(lambda x, c, z, y, dx=dx, dy=dy: (x - dx, c, z, y ^ dy))))
        gathered.append(same + [lax.ppermute(v, AX, perm(lambda x, c, z, y: (x, 1 - c, z, y))) for v in same])

    pre, hid = pl.pallas_call(
        functools.partial(hidden_kernel, n_x),
        out_shape=[
            jax.ShapeDtypeStruct((18 * full, 512), F32),
            jax.ShapeDtypeStruct((512, 16 * full), BF16),
        ],
        in_specs=[vmem] * (4 * n_x + 1),
        out_specs=[vmem] * 2,
        scratch_shapes=[pltpu.VMEM((3, 20, full, 512), BF16)],
        compiler_params=params(24),
        cost_estimate=cost(5),
        name="group_hidden",
    )(*gathered[0], first_weight)

    cot, mine, *sends = pl.pallas_call(
        functools.partial(gradient_kernel, n_x, n_z, groups, strip, block, scale),
        out_shape=[
            jax.ShapeDtypeStruct((3, 20, full, 512), BF16),
            jax.ShapeDtypeStruct((block, CH), F32),
        ]
        + [jax.ShapeDtypeStruct((block, CH), BF16)] * (n_z - 1),
        in_specs=[vmem] * (4 * n_x + 1),
        out_specs=[vmem] * (1 + n_z),
        scratch_shapes=[pltpu.VMEM((groups * 3 * CH + (0 if block % 8 == 0 else 16), CH), F32)],
        compiler_params=params(24),
        cost_estimate=cost(2),
        name="group_gradient",
    )(*gathered[1], hid)

    received = [
        lax.ppermute(v, AX, perm(lambda x, c, z, y, k=k: (x, c, z + k + 1, y))) for k, v in enumerate(sends)
    ]

    output, volume_grad = pl.pallas_call(
        local_kernel,
        out_shape=[jax.ShapeDtypeStruct((sy, sx, 512), BF16)] * 2,
        in_specs=[vmem] * 4,
        out_specs=[vmem] * 2,
        scratch_shapes=[
            pltpu.VMEM((3, 10, 16, 512), BF16),
            pltpu.VMEM((3, 12, 16, 512), BF16),
            pltpu.VMEM((3, 10, 16, 512), BF16),
            pltpu.VMEM((160, 512), F32),
        ],
        compiler_params=params(24),
        cost_estimate=cost(7),
        name="local_convolutions",
    )(pre, cot, first_weight, second_weight)

    def cells(v):
        return jnp.transpose(v.reshape(sy, sx, sz, chans), (1, 0, 2, 3))

    total = mine
    for v in received:
        total = total + v.astype(F32)
    return cells(output), cells(volume_grad), total.reshape(-1)


def solution(mesh):
    in_specs = (P("gx", "gy", None, None), P(), P(), P("gx", "gy", None, None))
    out_specs = (P("gx", "gy", None, None), P("gx", "gy", None, None), P(("gx", "gy")))
    return jax.shard_map(body, mesh=mesh, in_specs=in_specs, out_specs=out_specs, check_vma=False)
```

```python
import functools

import jax
import jax.numpy as jnp
from jax import lax
from jax.experimental import pallas as pl
from jax.experimental.pallas import tpu as pltpu
from jax.sharding import PartitionSpec as P

AX = ("gx", "gy")
F32 = jnp.float32
BF16 = jnp.bfloat16
CH = 256
ROWS = 27 * CH


def permutation(n_gx, n_gy, move):
    pairs = []
    for i in range(n_gx):
        for j in range(n_gy):
            x, c, z, y = move(i // 2, i % 2, j // 2, j % 2)
            x, z = x % (n_gx // 2), z % (n_gy // 2)
            pairs.append((i * n_gy + j, (x * 2 + c) * n_gy + z * 2 + y))
    return pairs


def dot(a, b):
    return lax.dot_general(a, b, (((1,), (0,)), ((), ())), preferred_element_type=F32)


def dot_t(a, b):
    return lax.dot_general(a, b, (((1,), (1,)), ((), ())), preferred_element_type=F32)


def shifted(v, by):
    if by == 0:
        return v
    axis, n = v.ndim - 2, v.shape[-2]
    if by > 0:
        parts = [lax.slice_in_dim(v, by, n, axis=axis), lax.slice_in_dim(v, 0, by, axis=axis)]
    else:
        parts = [lax.slice_in_dim(v, n + by, n, axis=axis), lax.slice_in_dim(v, 0, n + by, axis=axis)]
    return jnp.concatenate(parts, axis=axis)


def window(v, core):
    n = v.shape[-2]
    first = jnp.concatenate([v[..., n - 4 :, :], v[..., :12, :]], axis=-2)
    return jnp.where(core == 0, first, v[..., 4:20, :])


def ring(n_x, core, mine, theirs, rows):
    parts = []
    for dx in range(n_x):
        a, b = (ref[first : first + 16, :].astype(F32).reshape(2, 8, 512) for ref, first in (rows(mine, dx), rows(theirs, dx)))
        parts += [jnp.where(core == 0, a, b), jnp.where(core == 0, b, a)]
    return jnp.concatenate(parts, axis=1)


def assemble(n_x, which, pieces, put):
    _, core, _, side = place()
    n = 2 * n_x
    for dy in range(2):
        slot = side if dy == 0 else 1 - side
        for pair in range(4):
            rows = lambda refs, dx: (refs[dx * 2 + dy], which * 64 + pair * 16)
            put(which, 8 * slot + 2 * pair, ring(n_x, core, pieces[:n], pieces[n:], rows))


def putter(vol, cot):
    def put(which, row, line):
        for s in range(3):
            (vol, cot)[which][s, pl.ds(row, 2)] = shifted(line, (s - 1, 1 - s)[which]).astype(BF16)

    return put


def both(w):
    return jnp.concatenate([w[CH:], w[: 2 * CH]], axis=1)


def place():
    gx, gy = lax.axis_index("gx"), lax.axis_index("gy")
    return gx, lax.rem(gx, 2), lax.div(gy, 2), lax.rem(gy, 2)


def edge_kernel(n_x, *refs):
    *pieces, first = refs
    side = place()[3]
    for dx in range(n_x):
        for which in range(2):
            a, b = pieces[dx * 2], pieces[dx * 2 + 1]
            out = slice(dx * 32 + which * 16, dx * 32 + which * 16 + 16)
            rows = slice(which * 64, which * 64 + 16)
            first[out, :] = jnp.where(side == 0, a[rows, :], b[rows, :])


def later_kernel(lines, _, out):
    out[...] = lines[...]


def inner_kernel(n_x, *refs):
    *pieces, w_ref, pre, vol, cot = refs
    full = 16 * n_x
    put = putter(vol, cot)
    assemble(n_x, 0, pieces, put)
    for k in range(9):
        left = vol[k // 3, k % 3 : k % 3 + 14].reshape(14 * full, 512)
        term = dot(left, both(w_ref[k * 768 : k * 768 + 768, :]))
        pre[...] = term if k == 0 else pre[...] + term
    assemble(n_x, 1, pieces, put)


def gradient_kernel(n_x, n_z, groups, strip, block, scale, *refs):
    beyond_a, beyond_b, w_ref, pre, _, _, vol, cot, own_out, *sends, hid, grad, flat = refs
    gx, core, z, side = place()
    full = 16 * n_x
    put = putter(vol, cot)
    for which in range(2):
        put(which, 16, ring(n_x, core, beyond_a, beyond_b, lambda ref, dx: (ref, dx * 32 + which * 16)))
    outer = None
    for k in range(9):
        left = vol[k // 3, 14 + k % 3 : 16 + k % 3].reshape(2 * full, 512)
        term = dot(left, both(w_ref[k * 768 : k * 768 + 768, :]))
        outer = term if k == 0 else outer + term
    inner = jnp.concatenate([pre[...], outer], axis=0)
    hid[...] = (inner * jax.nn.sigmoid(inner)).T.astype(BF16)
    first = lax.div(gx * strip, 3 * CH)
    for k in range(groups):
        ab = jnp.minimum(first + k, 8)
        right = cot[lax.div(ab, 3), pl.ds(2 - lax.rem(ab, 3), 16)].reshape(16 * full, 512)
        product = dot(hid[...], right) * scale
        at = k * 3 * CH
        grad[at : at + CH, :] = product[:CH, CH:]
        grad[at + CH : at + 2 * CH, :] = product[:CH, :CH] + product[CH:, CH:]
        grad[at + 2 * CH : at + 3 * CH, :] = product[CH:, :CH]

    for k in range(n_z):
        start = gx * strip + (2 * lax.rem(z + k, n_z) + side) * block - first * 3 * CH
        if block % 8 == 0:
            value = grad[pl.ds(pl.multiple_of(start, 8), block), :]
        else:
            over = lax.rem(start, 8)
            rows = (block + 7 + 7) // 8 * 8
            value = grad[pl.ds(pl.multiple_of(start - over, 8), rows), :]
            value = pltpu.roll(value, lax.rem(rows - over, rows), 0)[:block]
        for half in range(2):
            flat[pl.ds(half, block, stride=2), :] = value[:, half * 128 : half * 128 + 128]
        if k == 0:
            own_out[...] = flat[...]
        else:
            sends[k - 1][...] = flat[...].astype(BF16)


def last_kernel(n_x, *refs):
    *pieces, out = refs
    _, core, _, side = place()
    n = 2 * n_x
    for which in range(2):
        low, high = (
            ring(n_x, core, pieces[:n], pieces[n:], lambda refs, dx: (refs[dx * 2 + dy], which * 64 + 48)) for dy in range(2)
        )
        lines = window(jnp.where(side == 0, high, low), core)
        out[which * 32 : which * 32 + 32, :] = lines.reshape(32, 512).astype(BF16)


def local_kernel(vol_ref, cot_ref, before_ref, w1, w2, out_ref, vgrad_ref, vol, hid, cot, thr, acc):
    _, core, _, side = place()

    def cut(which, ref):
        lines = window(ref[1, pl.ds(side * 8, 10)].astype(F32), core)
        before = before_ref[which * 32 : which * 32 + 32, :].astype(F32).reshape(2, 16, 512)
        before = jnp.where(side == 0, before, window(ref[1, 6:8].astype(F32), core))
        return jnp.concatenate([before, lines], axis=0)

    v, c = cut(0, vol_ref), cut(1, cot_ref)
    for s in range(3):
        vol[s] = shifted(v, s - 1).astype(BF16)
        cot[s] = shifted(c, s - 1).astype(BF16)

    for k in range(9):
        left = vol[k // 3, k % 3 : k % 3 + 10].reshape(160, 512)
        term = dot(left, both(w1[k * 768 : k * 768 + 768, :]))
        acc[...] = term if k == 0 else acc[...] + term
    pre = acc[...].reshape(10, 16, 512)
    sig = jax.nn.sigmoid(pre)
    for s in range(3):
        hid[s] = shifted(pre * sig, s - 1).astype(BF16)
    slope = sig * (1.0 + pre * (1.0 - sig))

    for k in range(9):
        left = cot[k // 3, k % 3 : k % 3 + 10].reshape(160, 512)
        term = dot_t(left, both(w2[(8 - k) * 768 : (8 - k) * 768 + 768, :]))
        acc[...] = term if k == 0 else acc[...] + term
    through = acc[...].reshape(10, 16, 512) * slope
    for s in range(3):
        thr[s] = shifted(through, s - 1).astype(BF16)

    for k in range(9):
        left = hid[k // 3, k % 3 : k % 3 + 8].reshape(128, 512)
        term = dot(left, both(w2[k * 768 : k * 768 + 768, :]))
        acc[:128] = term if k == 0 else acc[:128] + term
    out_ref[...] = acc[:128].reshape(8, 16, 512)[:, 4:12].astype(BF16)

    for k in range(9):
        left = thr[k // 3, k % 3 : k % 3 + 8].reshape(128, 512)
        term = dot_t(left, both(w1[(8 - k) * 768 : (8 - k) * 768 + 768, :]))
        acc[:128] = term if k == 0 else acc[:128] + term
    vgrad_ref[...] = acc[:128].reshape(8, 16, 512)[:, 4:12].astype(BF16)


def params(mib):
    return pltpu.CompilerParams(vmem_limit_bytes=mib * 1024 * 1024)


def cost(us):
    return pl.CostEstimate(flops=us * 10**9, bytes_accessed=us * 3 * 10**6, transcendentals=0)


def body(volume, first_weight, second_weight, cotangent):
    sx, sy, sz, chans = volume.shape
    n_gx, n_gy = lax.axis_size("gx"), lax.axis_size("gy")
    n_x, n_z = n_gx // 2, n_gy // 2
    scale = 1.0 / float(sx * n_gx * sy * n_gy * sz) ** 0.5
    strip = ROWS // n_gx
    block = strip // n_gy
    groups = max(-(-(i + 1) * strip // (3 * CH)) - i * strip // (3 * CH) for i in range(n_gx))
    full = sx * n_gx
    perm = functools.partial(permutation, n_gx, n_gy)
    vmem = pl.BlockSpec(memory_space=pltpu.VMEM)

    def lines(v):
        return jnp.transpose(v, (1, 0, 2, 3)).reshape(-1, sz * chans)

    def across(v):
        return lax.ppermute(v, AX, perm(lambda x, c, z, y: (x, 1 - c, z, y)))

    own = jnp.concatenate([lines(volume), lines(cotangent)])
    pieces = [own]
    for dx in range(n_x):
        for dy in range(2):
            if dx or dy:
                pieces.append(lax.ppermute(own, AX, perm(lambda x, c, z, y, dx=dx, dy=dy: (x - dx, c, z, y ^ dy))))
    first = pl.pallas_call(
        functools.partial(edge_kernel, n_x),
        out_shape=jax.ShapeDtypeStruct((n_x * 32, 512), BF16),
        in_specs=[vmem] * (2 * n_x),
        out_specs=vmem,
        compiler_params=params(4),
        cost_estimate=cost(4),
        name="edges",
    )(*pieces)
    pieces += [across(v) for v in pieces]
    beyond = lax.ppermute(first, AX, perm(lambda x, c, z, y: (x, c, z - 1, y)))

    last = pl.pallas_call(
        functools.partial(last_kernel, n_x),
        out_shape=jax.ShapeDtypeStruct((64, 512), BF16),
        in_specs=[vmem] * (4 * n_x),
        out_specs=vmem,
        compiler_params=params(4),
        cost_estimate=cost(0),
        name="last_lines",
    )(*pieces)
    before = lax.ppermute(last, AX, perm(lambda x, c, z, y: (x, c, z + 1, y)))

    plane = jax.ShapeDtypeStruct((3, 18, full, 512), BF16)
    pre, vol, cot = pl.pallas_call(
        functools.partial(inner_kernel, n_x),
        out_shape=[jax.ShapeDtypeStruct((14 * full, 512), F32), plane, plane],
        in_specs=[vmem] * (4 * n_x + 1),
        out_specs=[vmem] * 3,
        compiler_params=params(24),
        cost_estimate=cost(5),
        name="plane_inner",
    )(*pieces, first_weight)
    beyond = pl.pallas_call(
        later_kernel,
        out_shape=jax.ShapeDtypeStruct(beyond.shape, BF16),
        in_specs=[vmem] * 2,
        out_specs=vmem,
        compiler_params=params(4),
        cost_estimate=cost(0),
        name="later",
    )(beyond, pre)
    vol, cot, mine, *sends = pl.pallas_call(
        functools.partial(gradient_kernel, n_x, n_z, groups, strip, block, scale),
        out_shape=[plane, plane, jax.ShapeDtypeStruct((2 * block, 128), F32)]
        + [jax.ShapeDtypeStruct((2 * block, 128), BF16)] * (n_z - 1),
        in_specs=[vmem] * 6,
        out_specs=[vmem] * (2 + n_z),
        input_output_aliases={4: 0, 5: 1},
        scratch_shapes=[
            pltpu.VMEM((512, 16 * full), BF16),
            pltpu.VMEM((groups * 3 * CH + (0 if block % 8 == 0 else 16), CH), F32),
            pltpu.VMEM((2 * block, 128), F32),
        ],
        compiler_params=params(24),
        cost_estimate=cost(0),
        name="plane_gradient",
    )(beyond, across(beyond), first_weight, pre, vol, cot)

    received = [
        lax.ppermute(sends[k - 1], AX, perm(lambda x, c, z, y, k=k: (x, c, z + k, y)))
        for k in sorted(range(1, n_z), key=lambda k: k != n_z // 2)
    ]

    output, volume_grad = pl.pallas_call(
        local_kernel,
        out_shape=[jax.ShapeDtypeStruct((sy, sx, 512), BF16)] * 2,
        in_specs=[vmem] * 5,
        out_specs=[vmem] * 2,
        scratch_shapes=[
            pltpu.VMEM((3, 12, 16, 512), BF16),
            pltpu.VMEM((3, 10, 16, 512), BF16),
            pltpu.VMEM((3, 12, 16, 512), BF16),
            pltpu.VMEM((3, 10, 16, 512), BF16),
            pltpu.VMEM((160, 512), F32),
        ],
        compiler_params=params(24),
        cost_estimate=cost(0),
        name="local_convolutions",
    )(vol, cot, before, first_weight, second_weight)

    def cells(v):
        return jnp.transpose(v.reshape(sy, sx, sz, chans), (1, 0, 2, 3))

    total = mine
    for v in received:
        total = total + v.astype(F32)
    return cells(output), cells(volume_grad), total.reshape(-1)


def solution(mesh):
    in_specs = (P("gx", "gy", None, None), P(), P(), P("gx", "gy", None, None))
    out_specs = (P("gx", "gy", None, None), P("gx", "gy", None, None), P(("gx", "gy")))
    return jax.shard_map(body, mesh=mesh, in_specs=in_specs, out_specs=out_specs, check_vma=False)
```

```python
import functools

import jax
import jax.numpy as jnp
from jax import lax
from jax.experimental import pallas as pl
from jax.experimental.pallas import tpu as pltpu
from jax.sharding import PartitionSpec as P

AX = ("gx", "gy")
F32 = jnp.float32
BF16 = jnp.bfloat16
CH = 256
ROWS = 27 * CH


def permutation(n_gx, n_gy, move):
    pairs = []
    for i in range(n_gx):
        for j in range(n_gy):
            x, c, z, y = move(i // 2, i % 2, j // 2, j % 2)
            x, z = x % (n_gx // 2), z % (n_gy // 2)
            pairs.append((i * n_gy + j, (x * 2 + c) * n_gy + z * 2 + y))
    return pairs


def dot(a, b):
    return lax.dot_general(a, b, (((1,), (0,)), ((), ())), preferred_element_type=F32)


def dot_t(a, b):
    return lax.dot_general(a, b, (((1,), (1,)), ((), ())), preferred_element_type=F32)


def shifted(v, by):
    if by == 0:
        return v
    axis, n = v.ndim - 2, v.shape[-2]
    if by > 0:
        parts = [lax.slice_in_dim(v, by, n, axis=axis), lax.slice_in_dim(v, 0, by, axis=axis)]
    else:
        parts = [lax.slice_in_dim(v, n + by, n, axis=axis), lax.slice_in_dim(v, 0, n + by, axis=axis)]
    return jnp.concatenate(parts, axis=axis)


def window(v, core):
    n = v.shape[-2]
    first = jnp.concatenate([v[..., n - 4 :, :], v[..., :12, :]], axis=-2)
    return jnp.where(core == 0, first, v[..., 4:20, :])


def ring(n_x, core, mine, theirs, rows):
    parts = []
    for dx in range(n_x):
        a, b = (ref[first : first + 16, :].astype(F32).reshape(2, 8, 512) for ref, first in (rows(mine, dx), rows(theirs, dx)))
        parts += [jnp.where(core == 0, a, b), jnp.where(core == 0, b, a)]
    return jnp.concatenate(parts, axis=1)


def assemble(n_x, which, pieces, put):
    _, core, _, side = place()
    n = 2 * n_x
    for dy in range(2):
        slot = side if dy == 0 else 1 - side
        for pair in range(4):
            rows = lambda refs, dx: (refs[dx * 2 + dy], which * 64 + pair * 16)
            put(which, 2 + 8 * slot + 2 * pair, ring(n_x, core, pieces[:n], pieces[n:], rows))


def putter(vol, cot):
    def put(which, row, line):
        for s in range(3):
            (vol, cot)[which][s, pl.ds(row, 2)] = shifted(line, (s - 1, 1 - s)[which]).astype(BF16)

    return put


def both(w):
    return jnp.concatenate([w[CH:], w[: 2 * CH]], axis=1)


def place():
    gx, gy = lax.axis_index("gx"), lax.axis_index("gy")
    return gx, lax.rem(gx, 2), lax.div(gy, 2), lax.rem(gy, 2)


def edge_kernel(n_x, *refs):
    *pieces, last = refs
    side = place()[3]
    for dx in range(n_x):
        for which in range(2):
            a, b = pieces[dx * 2], pieces[dx * 2 + 1]
            out = slice(dx * 32 + which * 16, dx * 32 + which * 16 + 16)
            rows = slice(which * 64 + 48, which * 64 + 64)
            last[out, :] = jnp.where(side == 0, b[rows, :], a[rows, :])


def lines_kernel(fields, out, rows):
    sy, sx = rows.shape[:2]
    for k in range(2):
        for x in range(sx):
            block = fields[k, x].astype(F32)
            rows[:, x, :CH] = block[:, 0, :]
            rows[:, x, CH:] = block[:, 1, :]
        out[k * sy * sx : (k + 1) * sy * sx, :] = rows[...].reshape(sy * sx, 2 * CH).astype(BF16)


def later_kernel(lines, _, out):
    out[...] = lines[...]


def inner_kernel(n_x, *refs):
    *pieces, w_ref, pre, vol, cot = refs
    full = 16 * n_x
    put = putter(vol, cot)
    assemble(n_x, 0, pieces, put)
    for k in range(9):
        left = vol[k // 3, 2 + k % 3 : k % 3 + 16].reshape(14 * full, 512)
        term = dot(left, both(w_ref[k * 768 : k * 768 + 768, :]))
        pre[...] = term if k == 0 else pre[...] + term
    assemble(n_x, 1, pieces, put)


def gradient_kernel(n_x, n_z, groups, strip, block, scale, *refs):
    beyond_a, beyond_b, w_ref, pre, _, _, vol, cot, own_out, *sends, hid, grad, flat = refs
    gx, core, z, side = place()
    full = 16 * n_x
    put = putter(vol, cot)
    for which in range(2):
        put(which, 0, ring(n_x, core, beyond_a, beyond_b, lambda ref, dx: (ref, dx * 32 + which * 16)))
    outer = None
    for k in range(9):
        left = vol[k // 3, k % 3 : k % 3 + 2].reshape(2 * full, 512)
        term = dot(left, both(w_ref[k * 768 : k * 768 + 768, :]))
        outer = term if k == 0 else outer + term
    inner = jnp.concatenate([outer, pre[...]], axis=0)
    hid[...] = (inner * jax.nn.sigmoid(inner)).T.astype(BF16)
    first = lax.div(gx * strip, 3 * CH)
    for k in range(groups):
        ab = jnp.minimum(first + k, 8)
        right = cot[lax.div(ab, 3), pl.ds(2 - lax.rem(ab, 3), 16)].reshape(16 * full, 512)
        product = dot(hid[...], right) * scale
        at = k * 3 * CH
        grad[at : at + CH, :] = product[:CH, CH:]
        grad[at + CH : at + 2 * CH, :] = product[:CH, :CH] + product[CH:, CH:]
        grad[at + 2 * CH : at + 3 * CH, :] = product[CH:, :CH]

    for k in range(n_z):
        start = gx * strip + (2 * lax.rem(z + k, n_z) + side) * block - first * 3 * CH
        if block % 8 == 0:
            value = grad[pl.ds(pl.multiple_of(start, 8), block), :]
        else:
            over = lax.rem(start, 8)
            rows = (block + 7 + 7) // 8 * 8
            value = grad[pl.ds(pl.multiple_of(start - over, 8), rows), :]
            value = pltpu.roll(value, lax.rem(rows - over, rows), 0)[:block]
        for half in range(2):
            flat[pl.ds(half, block, stride=2), :] = value[:, half * 128 : half * 128 + 128]
        if k == 0:
            own_out[...] = flat[...]
        else:
            sends[k - 1][...] = flat[...].astype(BF16)


def first_kernel(n_x, *refs):
    *pieces, out = refs
    _, core, _, side = place()
    n = 2 * n_x
    for which in range(2):
        low, high = (
            ring(n_x, core, pieces[:n], pieces[n:], lambda refs, dx: (refs[dx * 2 + dy], which * 64)) for dy in range(2)
        )
        lines = window(jnp.where(side == 0, low, high), core)
        out[which * 32 : which * 32 + 32, :] = lines.reshape(32, 512).astype(BF16)


def local_kernel(vol_ref, cot_ref, after_ref, w1, w2, out_ref, vgrad_ref, vol, hid, cot, thr, acc):
    _, core, _, side = place()

    def cut(which, ref):
        lines = window(ref[1, pl.ds(side * 8, 10)].astype(F32), core)
        after = after_ref[which * 32 : which * 32 + 32, :].astype(F32).reshape(2, 16, 512)
        after = jnp.where(side == 0, window(ref[1, 10:12].astype(F32), core), after)
        return jnp.concatenate([lines, after], axis=0)

    v, c = cut(0, vol_ref), cut(1, cot_ref)
    for s in range(3):
        vol[s] = shifted(v, s - 1).astype(BF16)
        cot[s] = shifted(c, s - 1).astype(BF16)

    for k in range(9):
        left = vol[k // 3, k % 3 : k % 3 + 10].reshape(160, 512)
        term = dot(left, both(w1[k * 768 : k * 768 + 768, :]))
        acc[...] = term if k == 0 else acc[...] + term
    pre = acc[...].reshape(10, 16, 512)
    sig = jax.nn.sigmoid(pre)
    for s in range(3):
        hid[s] = shifted(pre * sig, s - 1).astype(BF16)
    slope = sig * (1.0 + pre * (1.0 - sig))

    for k in range(9):
        left = cot[k // 3, k % 3 : k % 3 + 10].reshape(160, 512)
        term = dot_t(left, both(w2[(8 - k) * 768 : (8 - k) * 768 + 768, :]))
        acc[...] = term if k == 0 else acc[...] + term
    through = acc[...].reshape(10, 16, 512) * slope
    for s in range(3):
        thr[s] = shifted(through, s - 1).astype(BF16)

    for k in range(9):
        left = hid[k // 3, k % 3 : k % 3 + 8].reshape(128, 512)
        term = dot(left, both(w2[k * 768 : k * 768 + 768, :]))
        acc[:128] = term if k == 0 else acc[:128] + term
    out_ref[...] = acc[:128].reshape(8, 16, 512)[:, 4:12].astype(BF16)

    for k in range(9):
        left = thr[k // 3, k % 3 : k % 3 + 8].reshape(128, 512)
        term = dot_t(left, both(w1[(8 - k) * 768 : (8 - k) * 768 + 768, :]))
        acc[:128] = term if k == 0 else acc[:128] + term
    vgrad_ref[...] = acc[:128].reshape(8, 16, 512)[:, 4:12].astype(BF16)


def params(mib):
    return pltpu.CompilerParams(vmem_limit_bytes=mib * 1024 * 1024)


def cost(us):
    return pl.CostEstimate(flops=us * 10**9, bytes_accessed=us * 3 * 10**6, transcendentals=0)


def body(volume, first_weight, second_weight, cotangent):
    sx, sy, sz, chans = volume.shape
    n_gx, n_gy = lax.axis_size("gx"), lax.axis_size("gy")
    n_x, n_z = n_gx // 2, n_gy // 2
    scale = 1.0 / float(sx * n_gx * sy * n_gy * sz) ** 0.5
    strip = ROWS // n_gx
    block = strip // n_gy
    groups = max(-(-(i + 1) * strip // (3 * CH)) - i * strip // (3 * CH) for i in range(n_gx))
    full = sx * n_gx
    perm = functools.partial(permutation, n_gx, n_gy)
    vmem = pl.BlockSpec(memory_space=pltpu.VMEM)

    def across(v):
        return lax.ppermute(v, AX, perm(lambda x, c, z, y: (x, 1 - c, z, y)))

    own = pl.pallas_call(
        lines_kernel,
        out_shape=jax.ShapeDtypeStruct((2 * sy * sx, sz * chans), BF16),
        in_specs=[vmem],
        out_specs=vmem,
        scratch_shapes=[pltpu.VMEM((sy, sx, sz * chans), F32)],
        compiler_params=params(4),
        cost_estimate=cost(1),
        name="lines",
    )(jnp.stack([volume, cotangent]))
    pieces = [own]
    for dx in range(n_x):
        for dy in range(2):
            if dx or dy:
                pieces.append(lax.ppermute(own, AX, perm(lambda x, c, z, y, dx=dx, dy=dy: (x - dx, c, z, y ^ dy))))
    last = pl.pallas_call(
        functools.partial(edge_kernel, n_x),
        out_shape=jax.ShapeDtypeStruct((n_x * 32, 512), BF16),
        in_specs=[vmem] * (2 * n_x),
        out_specs=vmem,
        compiler_params=params(4),
        cost_estimate=cost(4),
        name="edges",
    )(*pieces)
    pieces += [across(v) for v in pieces]
    beyond = lax.ppermute(last, AX, perm(lambda x, c, z, y: (x, c, z + 1, y)))

    first = pl.pallas_call(
        functools.partial(first_kernel, n_x),
        out_shape=jax.ShapeDtypeStruct((64, 512), BF16),
        in_specs=[vmem] * (4 * n_x),
        out_specs=vmem,
        compiler_params=params(4),
        cost_estimate=cost(0),
        name="first_lines",
    )(*pieces)
    after = lax.ppermute(first, AX, perm(lambda x, c, z, y: (x, c, z - 1, y)))

    plane = jax.ShapeDtypeStruct((3, 18, full, 512), BF16)
    pre, vol, cot = pl.pallas_call(
        functools.partial(inner_kernel, n_x),
        out_shape=[jax.ShapeDtypeStruct((14 * full, 512), F32), plane, plane],
        in_specs=[vmem] * (4 * n_x + 1),
        out_specs=[vmem] * 3,
        compiler_params=params(24),
        cost_estimate=cost(5),
        name="plane_inner",
    )(*pieces, first_weight)
    beyond = pl.pallas_call(
        later_kernel,
        out_shape=jax.ShapeDtypeStruct(beyond.shape, BF16),
        in_specs=[vmem] * 2,
        out_specs=vmem,
        compiler_params=params(4),
        cost_estimate=cost(0),
        name="later",
    )(beyond, pre)
    vol, cot, mine, *sends = pl.pallas_call(
        functools.partial(gradient_kernel, n_x, n_z, groups, strip, block, scale),
        out_shape=[plane, plane, jax.ShapeDtypeStruct((2 * block, 128), F32)]
        + [jax.ShapeDtypeStruct((2 * block, 128), BF16)] * (n_z - 1),
        in_specs=[vmem] * 6,
        out_specs=[vmem] * (2 + n_z),
        input_output_aliases={4: 0, 5: 1},
        scratch_shapes=[
            pltpu.VMEM((512, 16 * full), BF16),
            pltpu.VMEM((groups * 3 * CH + (0 if block % 8 == 0 else 16), CH), F32),
            pltpu.VMEM((2 * block, 128), F32),
        ],
        compiler_params=params(24),
        cost_estimate=cost(0),
        name="plane_gradient",
    )(beyond, across(beyond), first_weight, pre, vol, cot)

    received = [
        lax.ppermute(sends[k - 1], AX, perm(lambda x, c, z, y, k=k: (x, c, z + k, y)))
        for k in sorted(range(n_z - 1, 0, -1), key=lambda k: k != n_z // 2)
    ]

    output, volume_grad = pl.pallas_call(
        local_kernel,
        out_shape=[jax.ShapeDtypeStruct((sy, sx, 512), BF16)] * 2,
        in_specs=[vmem] * 5,
        out_specs=[vmem] * 2,
        scratch_shapes=[
            pltpu.VMEM((3, 12, 16, 512), BF16),
            pltpu.VMEM((3, 10, 16, 512), BF16),
            pltpu.VMEM((3, 12, 16, 512), BF16),
            pltpu.VMEM((3, 10, 16, 512), BF16),
            pltpu.VMEM((160, 512), F32),
        ],
        compiler_params=params(24),
        cost_estimate=cost(0),
        name="local_convolutions",
    )(vol, cot, after, first_weight, second_weight)

    def cells(v):
        return jnp.transpose(v.reshape(sy, sx, sz, chans), (1, 0, 2, 3))

    total = mine
    for v in received:
        total = total + v.astype(F32)
    return cells(output), cells(volume_grad), total.reshape(-1)


def solution(mesh):
    in_specs = (P("gx", "gy", None, None), P(), P(), P("gx", "gy", None, None))
    out_specs = (P("gx", "gy", None, None), P("gx", "gy", None, None), P(("gx", "gy")))
    return jax.shard_map(body, mesh=mesh, in_specs=in_specs, out_specs=out_specs, check_vma=False)
```

```python
import functools

import jax
import jax.numpy as jnp
from jax import lax
from jax.experimental import pallas as pl
from jax.experimental.pallas import tpu as pltpu
from jax.sharding import PartitionSpec as P

AX = ("gx", "gy")
F32 = jnp.float32
BF16 = jnp.bfloat16
CH = 256
ROWS = 27 * CH


def permutation(n_gx, n_gy, move):
    pairs = []
    for i in range(n_gx):
        for j in range(n_gy):
            x, c, z, y = move(i // 2, i % 2, j // 2, j % 2)
            x, z = x % (n_gx // 2), z % (n_gy // 2)
            pairs.append((i * n_gy + j, (x * 2 + c) * n_gy + z * 2 + y))
    return pairs


def dot(a, b):
    return lax.dot_general(a, b, (((1,), (0,)), ((), ())), preferred_element_type=F32)


def dot_t(a, b):
    return lax.dot_general(a, b, (((1,), (1,)), ((), ())), preferred_element_type=F32)


def shifted(v, by):
    if by == 0:
        return v
    axis, n = v.ndim - 2, v.shape[-2]
    if by > 0:
        parts = [lax.slice_in_dim(v, by, n, axis=axis), lax.slice_in_dim(v, 0, by, axis=axis)]
    else:
        parts = [lax.slice_in_dim(v, n + by, n, axis=axis), lax.slice_in_dim(v, 0, n + by, axis=axis)]
    return jnp.concatenate(parts, axis=axis)


def window(v, core):
    n = v.shape[-2]
    first = jnp.concatenate([v[..., n - 4 :, :], v[..., :12, :]], axis=-2)
    return jnp.where(core == 0, first, v[..., 4:20, :])


def ring(n_x, core, mine, theirs, rows):
    parts = []
    for dx in range(n_x):
        a, b = (ref[first : first + 16, :].astype(F32).reshape(2, 8, 512) for ref, first in (rows(mine, dx), rows(theirs, dx)))
        parts += [jnp.where(core == 0, a, b), jnp.where(core == 0, b, a)]
    return jnp.concatenate(parts, axis=1)


def assemble(n_x, which, pieces, put):
    _, core, _, side = place()
    n = 2 * n_x
    for dy in range(2):
        slot = side if dy == 0 else 1 - side
        for pair in range(4):
            rows = lambda refs, dx: (refs[dx * 2 + dy], which * 64 + pair * 16)
            put(which, 2 + 8 * slot + 2 * pair, ring(n_x, core, pieces[:n], pieces[n:], rows))


def putter(vol, cot):
    def put(which, row, line):
        for s in range(3):
            (vol, cot)[which][s, pl.ds(row, 2)] = shifted(line, (s - 1, 1 - s)[which]).astype(BF16)

    return put


def both(w):
    return jnp.concatenate([w[CH:], w[: 2 * CH]], axis=1)


def place():
    gx, gy = lax.axis_index("gx"), lax.axis_index("gy")
    return gx, lax.rem(gx, 2), lax.div(gy, 2), lax.rem(gy, 2)


def edge_kernel(n_x, *refs):
    *pieces, last = refs
    side = place()[3]
    for dx in range(n_x):
        for which in range(2):
            a, b = pieces[dx * 2], pieces[dx * 2 + 1]
            out = slice(dx * 32 + which * 16, dx * 32 + which * 16 + 16)
            rows = slice(which * 64 + 48, which * 64 + 64)
            last[out, :] = jnp.where(side == 0, b[rows, :], a[rows, :])


def lines_kernel(fields, out, rows):
    sy, sx = rows.shape[:2]
    for k in range(2):
        for x in range(sx):
            block = fields[k, x].astype(F32)
            rows[:, x, :CH] = block[:, 0, :]
            rows[:, x, CH:] = block[:, 1, :]
        out[k * sy * sx : (k + 1) * sy * sx, :] = rows[...].reshape(sy * sx, 2 * CH).astype(BF16)


def later_kernel(lines, _, out):
    out[...] = lines[...]


def silu_t(pre):
    return (pre * jax.nn.sigmoid(pre)).T.astype(BF16)


def inner_kernel(n_x, *refs):
    *pieces, w_ref, outer, hid, vol, cot, pre = refs
    full = 16 * n_x
    put = putter(vol, cot)
    vol[:, :2] = jnp.zeros_like(vol[:, :2])
    assemble(n_x, 0, pieces, put)
    for k in range(9):
        left = vol[k // 3, k % 3 : k % 3 + 16].reshape(16 * full, 512)
        term = dot(left, both(w_ref[k * 768 : k * 768 + 768, :]))
        pre[...] = term if k == 0 else pre[...] + term
    outer[...] = pre[: 2 * full, :]
    hid[:, : 14 * full] = silu_t(pre[2 * full :, :])
    assemble(n_x, 1, pieces, put)


def gradient_kernel(n_x, n_z, groups, strip, block, scale, *refs):
    beyond_a, beyond_b, w_ref, outer, _, _, _, vol, cot, hid, own_out, *sends, grad, flat = refs
    gx, core, z, side = place()
    full = 16 * n_x
    put = putter(vol, cot)
    for which in range(2):
        put(which, 0, ring(n_x, core, beyond_a, beyond_b, lambda ref, dx: (ref, dx * 32 + which * 16)))
    pre, first_line = outer[...], None
    for a in range(3):
        left = vol[a, 0:2].reshape(2 * full, 512)
        w = w_ref[a * 2304 : a * 2304 + 1536, :]
        pre = pre + dot(left, both(w[:768]))
        term = dot(left[full:], both(w[768:]))
        first_line = term if a == 0 else first_line + term
    pre = jnp.concatenate([pre[:full] + first_line, pre[full:]], axis=0)
    hid[:, 14 * full :] = silu_t(pre)
    first = lax.div(gx * strip, 3 * CH)
    for k in range(groups):
        ab = jnp.minimum(first + k, 8)
        shift, row = lax.div(ab, 3), 2 - lax.rem(ab, 3)
        right = jnp.concatenate([cot[shift, pl.ds(row + 2, 14)], cot[shift, pl.ds(row, 2)]], axis=0).reshape(16 * full, 512)
        product = dot(hid[...], right) * scale
        at = k * 3 * CH
        grad[at : at + CH, :] = product[:CH, CH:]
        grad[at + CH : at + 2 * CH, :] = product[:CH, :CH] + product[CH:, CH:]
        grad[at + 2 * CH : at + 3 * CH, :] = product[CH:, :CH]

    for k in range(n_z):
        start = gx * strip + (2 * lax.rem(z + k, n_z) + side) * block - first * 3 * CH
        if block % 8 == 0:
            value = grad[pl.ds(pl.multiple_of(start, 8), block), :]
        else:
            over = lax.rem(start, 8)
            rows = (block + 7 + 7) // 8 * 8
            value = grad[pl.ds(pl.multiple_of(start - over, 8), rows), :]
            value = pltpu.roll(value, lax.rem(rows - over, rows), 0)[:block]
        for half in range(2):
            flat[pl.ds(half, block, stride=2), :] = value[:, half * 128 : half * 128 + 128]
        if k == 0:
            own_out[...] = flat[...]
        else:
            sends[k - 1][...] = flat[...].astype(BF16)


def first_kernel(n_x, *refs):
    *pieces, out = refs
    _, core, _, side = place()
    n = 2 * n_x
    for which in range(2):
        low, high = (
            ring(n_x, core, pieces[:n], pieces[n:], lambda refs, dx: (refs[dx * 2 + dy], which * 64)) for dy in range(2)
        )
        lines = window(jnp.where(side == 0, low, high), core)
        out[which * 32 : which * 32 + 32, :] = lines.reshape(32, 512).astype(BF16)


def local_kernel(vol_ref, cot_ref, after_ref, w1, w2, out_ref, vgrad_ref, vol, hid, cot, thr, acc):
    _, core, _, side = place()

    def cut(which, ref):
        lines = window(ref[1, pl.ds(side * 8, 10)].astype(F32), core)
        after = after_ref[which * 32 : which * 32 + 32, :].astype(F32).reshape(2, 16, 512)
        after = jnp.where(side == 0, window(ref[1, 10:12].astype(F32), core), after)
        return jnp.concatenate([lines, after], axis=0)

    v, c = cut(0, vol_ref), cut(1, cot_ref)
    for s in range(3):
        vol[s] = shifted(v, s - 1).astype(BF16)
        cot[s] = shifted(c, s - 1).astype(BF16)

    for k in range(9):
        left = vol[k // 3, k % 3 : k % 3 + 10].reshape(160, 512)
        term = dot(left, both(w1[k * 768 : k * 768 + 768, :]))
        acc[...] = term if k == 0 else acc[...] + term
    pre = acc[...].reshape(10, 16, 512)
    sig = jax.nn.sigmoid(pre)
    for s in range(3):
        hid[s] = shifted(pre * sig, s - 1).astype(BF16)
    slope = sig * (1.0 + pre * (1.0 - sig))

    for k in range(9):
        left = cot[k // 3, k % 3 : k % 3 + 10].reshape(160, 512)
        term = dot_t(left, both(w2[(8 - k) * 768 : (8 - k) * 768 + 768, :]))
        acc[...] = term if k == 0 else acc[...] + term
    through = acc[...].reshape(10, 16, 512) * slope
    for s in range(3):
        thr[s] = shifted(through, s - 1).astype(BF16)

    for k in range(9):
        left = hid[k // 3, k % 3 : k % 3 + 8].reshape(128, 512)
        term = dot(left, both(w2[k * 768 : k * 768 + 768, :]))
        acc[:128] = term if k == 0 else acc[:128] + term
    out_ref[...] = acc[:128].reshape(8, 16, 512)[:, 4:12].astype(BF16)

    for k in range(9):
        left = thr[k // 3, k % 3 : k % 3 + 8].reshape(128, 512)
        term = dot_t(left, both(w1[(8 - k) * 768 : (8 - k) * 768 + 768, :]))
        acc[:128] = term if k == 0 else acc[:128] + term
    vgrad_ref[...] = acc[:128].reshape(8, 16, 512)[:, 4:12].astype(BF16)


def params(mib):
    return pltpu.CompilerParams(vmem_limit_bytes=mib * 1024 * 1024)


def cost(us):
    return pl.CostEstimate(flops=us * 10**9, bytes_accessed=us * 3 * 10**6, transcendentals=0)


def body(volume, first_weight, second_weight, cotangent):
    sx, sy, sz, chans = volume.shape
    n_gx, n_gy = lax.axis_size("gx"), lax.axis_size("gy")
    n_x, n_z = n_gx // 2, n_gy // 2
    scale = 1.0 / float(sx * n_gx * sy * n_gy * sz) ** 0.5
    strip = ROWS // n_gx
    block = strip // n_gy
    groups = max(-(-(i + 1) * strip // (3 * CH)) - i * strip // (3 * CH) for i in range(n_gx))
    full = sx * n_gx
    perm = functools.partial(permutation, n_gx, n_gy)
    vmem = pl.BlockSpec(memory_space=pltpu.VMEM)

    def across(v):
        return lax.ppermute(v, AX, perm(lambda x, c, z, y: (x, 1 - c, z, y)))

    own = pl.pallas_call(
        lines_kernel,
        out_shape=jax.ShapeDtypeStruct((2 * sy * sx, sz * chans), BF16),
        in_specs=[vmem],
        out_specs=vmem,
        scratch_shapes=[pltpu.VMEM((sy, sx, sz * chans), F32)],
        compiler_params=params(4),
        cost_estimate=cost(1),
        name="lines",
    )(jnp.stack([volume, cotangent]))
    pieces = [own]
    for dx in range(n_x):
        for dy in range(2):
            if dx or dy:
                pieces.append(lax.ppermute(own, AX, perm(lambda x, c, z, y, dx=dx, dy=dy: (x - dx, c, z, y ^ dy))))
    last = pl.pallas_call(
        functools.partial(edge_kernel, n_x),
        out_shape=jax.ShapeDtypeStruct((n_x * 32, 512), BF16),
        in_specs=[vmem] * (2 * n_x),
        out_specs=vmem,
        compiler_params=params(4),
        cost_estimate=cost(4),
        name="edges",
    )(*pieces)
    pieces += [across(v) for v in pieces]
    beyond = lax.ppermute(last, AX, perm(lambda x, c, z, y: (x, c, z + 1, y)))

    first = pl.pallas_call(
        functools.partial(first_kernel, n_x),
        out_shape=jax.ShapeDtypeStruct((64, 512), BF16),
        in_specs=[vmem] * (4 * n_x),
        out_specs=vmem,
        compiler_params=params(4),
        cost_estimate=cost(0),
        name="first_lines",
    )(*pieces)
    after = lax.ppermute(first, AX, perm(lambda x, c, z, y: (x, c, z - 1, y)))

    plane = jax.ShapeDtypeStruct((3, 18, full, 512), BF16)
    columns = jax.ShapeDtypeStruct((512, 16 * full), BF16)
    outer, hid, vol, cot = pl.pallas_call(
        functools.partial(inner_kernel, n_x),
        out_shape=[jax.ShapeDtypeStruct((2 * full, 512), F32), columns, plane, plane],
        in_specs=[vmem] * (4 * n_x + 1),
        out_specs=[vmem] * 4,
        scratch_shapes=[pltpu.VMEM((16 * full, 512), F32)],
        compiler_params=params(24),
        cost_estimate=cost(5),
        name="plane_inner",
    )(*pieces, first_weight)
    beyond = pl.pallas_call(
        later_kernel,
        out_shape=jax.ShapeDtypeStruct(beyond.shape, BF16),
        in_specs=[vmem] * 2,
        out_specs=vmem,
        compiler_params=params(4),
        cost_estimate=cost(0),
        name="later",
    )(beyond, outer)
    vol, cot, _, mine, *sends = pl.pallas_call(
        functools.partial(gradient_kernel, n_x, n_z, groups, strip, block, scale),
        out_shape=[plane, plane, columns, jax.ShapeDtypeStruct((2 * block, 128), F32)]
        + [jax.ShapeDtypeStruct((2 * block, 128), BF16)] * (n_z - 1),
        in_specs=[vmem] * 7,
        out_specs=[vmem] * (3 + n_z),
        input_output_aliases={4: 0, 5: 1, 6: 2},
        scratch_shapes=[
            pltpu.VMEM((groups * 3 * CH + (0 if block % 8 == 0 else 16), CH), F32),
            pltpu.VMEM((2 * block, 128), F32),
        ],
        compiler_params=params(24),
        cost_estimate=cost(0),
        name="plane_gradient",
    )(beyond, across(beyond), first_weight, outer, vol, cot, hid)

    received = [
        lax.ppermute(sends[k - 1], AX, perm(lambda x, c, z, y, k=k: (x, c, z + k, y)))
        for k in sorted(range(n_z - 1, 0, -1), key=lambda k: k != n_z // 2)
    ]

    output, volume_grad = pl.pallas_call(
        local_kernel,
        out_shape=[jax.ShapeDtypeStruct((sy, sx, 512), BF16)] * 2,
        in_specs=[vmem] * 5,
        out_specs=[vmem] * 2,
        scratch_shapes=[
            pltpu.VMEM((3, 12, 16, 512), BF16),
            pltpu.VMEM((3, 10, 16, 512), BF16),
            pltpu.VMEM((3, 12, 16, 512), BF16),
            pltpu.VMEM((3, 10, 16, 512), BF16),
            pltpu.VMEM((160, 512), F32),
        ],
        compiler_params=params(24),
        cost_estimate=cost(0),
        name="local_convolutions",
    )(vol, cot, after, first_weight, second_weight)

    def cells(v):
        return jnp.transpose(v.reshape(sy, sx, sz, chans), (1, 0, 2, 3))

    total = mine
    for v in received:
        total = total + v.astype(F32)
    return cells(output), cells(volume_grad), total.reshape(-1)


def solution(mesh):
    in_specs = (P("gx", "gy", None, None), P(), P(), P("gx", "gy", None, None))
    out_specs = (P("gx", "gy", None, None), P("gx", "gy", None, None), P(("gx", "gy")))
    return jax.shard_map(body, mesh=mesh, in_specs=in_specs, out_specs=out_specs, check_vma=False)
```

```python
import functools

import jax
import jax.numpy as jnp
from jax import lax
from jax.experimental import pallas as pl
from jax.experimental.pallas import tpu as pltpu
from jax.sharding import PartitionSpec as P

AX = ("gx", "gy")
F32 = jnp.float32
BF16 = jnp.bfloat16
CH = 256
ROWS = 27 * CH


def permutation(n_gx, n_gy, move):
    pairs = []
    for i in range(n_gx):
        for j in range(n_gy):
            x, c, z, y = move(i // 2, i % 2, j // 2, j % 2)
            x, z = x % (n_gx // 2), z % (n_gy // 2)
            pairs.append((i * n_gy + j, (x * 2 + c) * n_gy + z * 2 + y))
    return pairs


def dot(a, b):
    return lax.dot_general(a, b, (((1,), (0,)), ((), ())), preferred_element_type=F32)


def dot_t(a, b):
    return lax.dot_general(a, b, (((1,), (1,)), ((), ())), preferred_element_type=F32)


def shifted(v, by):
    if by == 0:
        return v
    axis, n = v.ndim - 2, v.shape[-2]
    if by > 0:
        parts = [lax.slice_in_dim(v, by, n, axis=axis), lax.slice_in_dim(v, 0, by, axis=axis)]
    else:
        parts = [lax.slice_in_dim(v, n + by, n, axis=axis), lax.slice_in_dim(v, 0, n + by, axis=axis)]
    return jnp.concatenate(parts, axis=axis)


def window(v, core):
    n = v.shape[-2]
    first = jnp.concatenate([v[..., n - 4 :, :], v[..., :12, :]], axis=-2)
    return jnp.where(core == 0, first, v[..., 4:20, :])


def ring(n_x, core, mine, theirs, rows):
    parts = []
    for dx in range(n_x):
        a, b = (ref[first : first + 16, :].astype(F32).reshape(2, 8, 512) for ref, first in (rows(mine, dx), rows(theirs, dx)))
        parts += [jnp.where(core == 0, a, b), jnp.where(core == 0, b, a)]
    return jnp.concatenate(parts, axis=1)


def assemble(n_x, which, pieces, put):
    _, core, _, side = place()
    n = 2 * n_x
    for dy in range(2):
        slot = side if dy == 0 else 1 - side
        for pair in range(4):
            rows = lambda refs, dx: (refs[dx * 2 + dy], which * 64 + pair * 16)
            put(which, 2 + 8 * slot + 2 * pair, ring(n_x, core, pieces[:n], pieces[n:], rows))


def putter(vol, cot):
    def put(which, row, line):
        for s in range(3):
            (vol, cot)[which][s, pl.ds(row, 2)] = shifted(line, (s - 1, 1 - s)[which]).astype(BF16)

    return put


def both(w):
    return jnp.concatenate([w[CH:], w[: 2 * CH]], axis=1)


def place():
    gx, gy = lax.axis_index("gx"), lax.axis_index("gy")
    return gx, lax.rem(gx, 2), lax.div(gy, 2), lax.rem(gy, 2)


def edge_kernel(n_x, *refs):
    *pieces, last = refs
    side = place()[3]
    for dx in range(n_x):
        for which in range(2):
            a, b = pieces[dx * 2], pieces[dx * 2 + 1]
            out = slice(dx * 32 + which * 16, dx * 32 + which * 16 + 16)
            rows = slice(which * 64 + 48, which * 64 + 64)
            last[out, :] = jnp.where(side == 0, b[rows, :], a[rows, :])


def lines_kernel(fields, out, rows):
    sy, sx = rows.shape[:2]
    for k in range(2):
        for x in range(sx):
            block = fields[k, x].astype(F32)
            rows[:, x, :CH] = block[:, 0, :]
            rows[:, x, CH:] = block[:, 1, :]
        out[k * sy * sx : (k + 1) * sy * sx, :] = rows[...].reshape(sy * sx, 2 * CH).astype(BF16)


def later_kernel(lines, _, out):
    out[...] = lines[...]


def silu_t(pre):
    return (pre * jax.nn.sigmoid(pre)).T.astype(BF16)


def inner_kernel(n_x, *refs):
    *pieces, w_ref, outer, hid, vol, cot, pre = refs
    full = 16 * n_x
    put = putter(vol, cot)
    vol[:, :2] = jnp.zeros_like(vol[:, :2])
    assemble(n_x, 0, pieces, put)
    for k in range(9):
        left = vol[k // 3, k % 3 : k % 3 + 16].reshape(16 * full, 512)
        term = dot(left, both(w_ref[k * 768 : k * 768 + 768, :]))
        pre[...] = term if k == 0 else pre[...] + term
    outer[...] = pre[: 2 * full, :]
    hid[:, : 14 * full] = silu_t(pre[2 * full :, :])
    assemble(n_x, 1, pieces, put)


def gradient_kernel(n_x, n_z, groups, strip, block, scale, *refs):
    beyond_a, beyond_b, w_ref, outer, cot, hid_ref, near_vol, near_cot, own_out, *sends, hid, ends, grad, flat = refs
    gx, core, z, side = place()
    full = 16 * n_x
    put = putter(near_vol, near_cot)
    for which in range(2):
        put(which, 0, ring(n_x, core, beyond_a, beyond_b, lambda ref, dx: (ref, dx * 32 + which * 16)))
    ends[:, :2] = near_cot[...]
    ends[:, 2:] = cot[:, 2:4]
    pre, first_line = outer[...], None
    for a in range(3):
        left = near_vol[a].reshape(2 * full, 512)
        w = w_ref[a * 2304 : a * 2304 + 1536, :]
        pre = pre + dot(left, both(w[:768]))
        term = dot(left[full:], both(w[768:]))
        first_line = term if a == 0 else first_line + term
    pre = jnp.concatenate([pre[:full] + first_line, pre[full:]], axis=0)
    hid[...] = hid_ref[...]
    hid[:, 14 * full :] = silu_t(pre)
    first = lax.div(gx * strip, 3 * CH)
    for k in range(groups):
        ab = jnp.minimum(first + k, 8)
        shift, row = lax.div(ab, 3), 2 - lax.rem(ab, 3)
        right = jnp.concatenate([cot[shift, pl.ds(row + 2, 14)], ends[shift, pl.ds(row, 2)]], axis=0).reshape(16 * full, 512)
        product = dot(hid[...], right) * scale
        at = k * 3 * CH
        grad[at : at + CH, :] = product[:CH, CH:]
        grad[at + CH : at + 2 * CH, :] = product[:CH, :CH] + product[CH:, CH:]
        grad[at + 2 * CH : at + 3 * CH, :] = product[CH:, :CH]

    for k in range(n_z):
        start = gx * strip + (2 * lax.rem(z + k, n_z) + side) * block - first * 3 * CH
        if block % 8 == 0:
            value = grad[pl.ds(pl.multiple_of(start, 8), block), :]
        else:
            over = lax.rem(start, 8)
            rows = (block + 7 + 7) // 8 * 8
            value = grad[pl.ds(pl.multiple_of(start - over, 8), rows), :]
            value = pltpu.roll(value, lax.rem(rows - over, rows), 0)[:block]
        for half in range(2):
            flat[pl.ds(half, block, stride=2), :] = value[:, half * 128 : half * 128 + 128]
        if k == 0:
            own_out[...] = flat[...]
        else:
            sends[k - 1][...] = flat[...].astype(BF16)


def first_kernel(n_x, *refs):
    *pieces, out = refs
    _, core, _, side = place()
    n = 2 * n_x
    for which in range(2):
        low, high = (
            ring(n_x, core, pieces[:n], pieces[n:], lambda refs, dx: (refs[dx * 2 + dy], which * 64)) for dy in range(2)
        )
        lines = window(jnp.where(side == 0, low, high), core)
        out[which * 32 : which * 32 + 32, :] = lines.reshape(32, 512).astype(BF16)


def local_kernel(vol_ref, cot_ref, near_vol, near_cot, after_ref, w1, w2, out_ref, vgrad_ref, vol, hid, cot, thr, acc):
    _, core, _, side = place()

    def cut(which, ref, near):
        before = jnp.where(side == 0, near[1].astype(F32), ref[1, 8:10].astype(F32))
        lines = [before, ref[1, pl.ds(2 + side * 8, 8)].astype(F32)]
        after = after_ref[which * 32 : which * 32 + 32, :].astype(F32).reshape(2, 16, 512)
        after = jnp.where(side == 0, window(ref[1, 10:12].astype(F32), core), after)
        return jnp.concatenate([window(jnp.concatenate(lines, axis=0), core), after], axis=0)

    v, c = cut(0, vol_ref, near_vol), cut(1, cot_ref, near_cot)
    for s in range(3):
        vol[s] = shifted(v, s - 1).astype(BF16)
        cot[s] = shifted(c, s - 1).astype(BF16)

    for k in range(9):
        left = vol[k // 3, k % 3 : k % 3 + 10].reshape(160, 512)
        term = dot(left, both(w1[k * 768 : k * 768 + 768, :]))
        acc[...] = term if k == 0 else acc[...] + term
    pre = acc[...].reshape(10, 16, 512)
    sig = jax.nn.sigmoid(pre)
    for s in range(3):
        hid[s] = shifted(pre * sig, s - 1).astype(BF16)
    slope = sig * (1.0 + pre * (1.0 - sig))

    for k in range(9):
        left = cot[k // 3, k % 3 : k % 3 + 10].reshape(160, 512)
        term = dot_t(left, both(w2[(8 - k) * 768 : (8 - k) * 768 + 768, :]))
        acc[...] = term if k == 0 else acc[...] + term
    through = acc[...].reshape(10, 16, 512) * slope
    for s in range(3):
        thr[s] = shifted(through, s - 1).astype(BF16)

    for k in range(9):
        left = hid[k // 3, k % 3 : k % 3 + 8].reshape(128, 512)
        term = dot(left, both(w2[k * 768 : k * 768 + 768, :]))
        acc[:128] = term if k == 0 else acc[:128] + term
    out_ref[...] = acc[:128].reshape(8, 16, 512)[:, 4:12].astype(BF16)

    for k in range(9):
        left = thr[k // 3, k % 3 : k % 3 + 8].reshape(128, 512)
        term = dot_t(left, both(w1[(8 - k) * 768 : (8 - k) * 768 + 768, :]))
        acc[:128] = term if k == 0 else acc[:128] + term
    vgrad_ref[...] = acc[:128].reshape(8, 16, 512)[:, 4:12].astype(BF16)


def params(mib):
    return pltpu.CompilerParams(vmem_limit_bytes=mib * 1024 * 1024)


def cost(us):
    return pl.CostEstimate(flops=us * 10**9, bytes_accessed=us * 3 * 10**6, transcendentals=0)


def body(volume, first_weight, second_weight, cotangent):
    sx, sy, sz, chans = volume.shape
    n_gx, n_gy = lax.axis_size("gx"), lax.axis_size("gy")
    n_x, n_z = n_gx // 2, n_gy // 2
    scale = 1.0 / float(sx * n_gx * sy * n_gy * sz) ** 0.5
    strip = ROWS // n_gx
    block = strip // n_gy
    groups = max(-(-(i + 1) * strip // (3 * CH)) - i * strip // (3 * CH) for i in range(n_gx))
    full = sx * n_gx
    perm = functools.partial(permutation, n_gx, n_gy)
    vmem = pl.BlockSpec(memory_space=pltpu.VMEM)

    def across(v):
        return lax.ppermute(v, AX, perm(lambda x, c, z, y: (x, 1 - c, z, y)))

    own = pl.pallas_call(
        lines_kernel,
        out_shape=jax.ShapeDtypeStruct((2 * sy * sx, sz * chans), BF16),
        in_specs=[vmem],
        out_specs=vmem,
        scratch_shapes=[pltpu.VMEM((sy, sx, sz * chans), F32)],
        compiler_params=params(4),
        cost_estimate=cost(1),
        name="lines",
    )(jnp.stack([volume, cotangent]))
    pieces = [own]
    for dx in range(n_x):
        for dy in range(2):
            if dx or dy:
                pieces.append(lax.ppermute(own, AX, perm(lambda x, c, z, y, dx=dx, dy=dy: (x - dx, c, z, y ^ dy))))
    last = pl.pallas_call(
        functools.partial(edge_kernel, n_x),
        out_shape=jax.ShapeDtypeStruct((n_x * 32, 512), BF16),
        in_specs=[vmem] * (2 * n_x),
        out_specs=vmem,
        compiler_params=params(4),
        cost_estimate=cost(4),
        name="edges",
    )(*pieces)
    pieces += [across(v) for v in pieces]
    beyond = lax.ppermute(last, AX, perm(lambda x, c, z, y: (x, c, z + 1, y)))

    first = pl.pallas_call(
        functools.partial(first_kernel, n_x),
        out_shape=jax.ShapeDtypeStruct((64, 512), BF16),
        in_specs=[vmem] * (4 * n_x),
        out_specs=vmem,
        compiler_params=params(4),
        cost_estimate=cost(0),
        name="first_lines",
    )(*pieces)
    after = lax.ppermute(first, AX, perm(lambda x, c, z, y: (x, c, z - 1, y)))

    plane = jax.ShapeDtypeStruct((3, 18, full, 512), BF16)
    columns = jax.ShapeDtypeStruct((512, 16 * full), BF16)
    outer, hid, vol, cot = pl.pallas_call(
        functools.partial(inner_kernel, n_x),
        out_shape=[jax.ShapeDtypeStruct((2 * full, 512), F32), columns, plane, plane],
        in_specs=[vmem] * (4 * n_x + 1),
        out_specs=[vmem] * 4,
        scratch_shapes=[pltpu.VMEM((16 * full, 512), F32)],
        compiler_params=params(24),
        cost_estimate=cost(5),
        name="plane_inner",
    )(*pieces, first_weight)
    beyond = pl.pallas_call(
        later_kernel,
        out_shape=jax.ShapeDtypeStruct(beyond.shape, BF16),
        in_specs=[vmem] * 2,
        out_specs=vmem,
        compiler_params=params(4),
        cost_estimate=cost(0),
        name="later",
    )(beyond, outer)
    near = jax.ShapeDtypeStruct((3, 2, full, 512), BF16)
    near_vol, near_cot, mine, *sends = pl.pallas_call(
        functools.partial(gradient_kernel, n_x, n_z, groups, strip, block, scale),
        out_shape=[near, near, jax.ShapeDtypeStruct((2 * block, 128), F32)]
        + [jax.ShapeDtypeStruct((2 * block, 128), BF16)] * (n_z - 1),
        in_specs=[vmem] * 6,
        out_specs=[vmem] * (2 + n_z),
        scratch_shapes=[
            pltpu.VMEM((512, 16 * full), BF16),
            pltpu.VMEM((3, 4, full, 512), BF16),
            pltpu.VMEM((groups * 3 * CH + (0 if block % 8 == 0 else 16), CH), F32),
            pltpu.VMEM((2 * block, 128), F32),
        ],
        compiler_params=params(24),
        cost_estimate=cost(0),
        name="plane_gradient",
    )(beyond, across(beyond), first_weight, outer, cot, hid)

    received = [
        lax.ppermute(sends[k - 1], AX, perm(lambda x, c, z, y, k=k: (x, c, z + k, y)))
        for k in sorted(range(n_z - 1, 0, -1), key=lambda k: k != n_z // 2)
    ]

    output, volume_grad = pl.pallas_call(
        local_kernel,
        out_shape=[jax.ShapeDtypeStruct((sy, sx, 512), BF16)] * 2,
        in_specs=[vmem] * 7,
        out_specs=[vmem] * 2,
        scratch_shapes=[
            pltpu.VMEM((3, 12, 16, 512), BF16),
            pltpu.VMEM((3, 10, 16, 512), BF16),
            pltpu.VMEM((3, 12, 16, 512), BF16),
            pltpu.VMEM((3, 10, 16, 512), BF16),
            pltpu.VMEM((160, 512), F32),
        ],
        compiler_params=params(24),
        cost_estimate=cost(0),
        name="local_convolutions",
    )(vol, cot, near_vol, near_cot, after, first_weight, second_weight)

    def cells(v):
        return jnp.transpose(v.reshape(sy, sx, sz, chans), (1, 0, 2, 3))

    total = mine
    for v in received:
        total = total + v.astype(F32)
    return cells(output), cells(volume_grad), total.reshape(-1)


def solution(mesh):
    in_specs = (P("gx", "gy", None, None), P(), P(), P("gx", "gy", None, None))
    out_specs = (P("gx", "gy", None, None), P("gx", "gy", None, None), P(("gx", "gy")))
    return jax.shard_map(body, mesh=mesh, in_specs=in_specs, out_specs=out_specs, check_vma=False)
```

```python
import functools

import jax
import jax.numpy as jnp
from jax import lax
from jax.experimental import pallas as pl
from jax.experimental.pallas import tpu as pltpu
from jax.sharding import PartitionSpec as P

AX = ("gx", "gy")
F32 = jnp.float32
BF16 = jnp.bfloat16
CH = 256
ROWS = 27 * CH


def permutation(n_gx, n_gy, move):
    pairs = []
    for i in range(n_gx):
        for j in range(n_gy):
            x, c, z, y = move(i // 2, i % 2, j // 2, j % 2)
            x, z = x % (n_gx // 2), z % (n_gy // 2)
            pairs.append((i * n_gy + j, (x * 2 + c) * n_gy + z * 2 + y))
    return pairs


def dot(a, b):
    return lax.dot_general(a, b, (((1,), (0,)), ((), ())), preferred_element_type=F32)


def dot_t(a, b):
    return lax.dot_general(a, b, (((1,), (1,)), ((), ())), preferred_element_type=F32)


def shifted(v, by):
    if by == 0:
        return v
    axis, n = v.ndim - 2, v.shape[-2]
    if by > 0:
        parts = [lax.slice_in_dim(v, by, n, axis=axis), lax.slice_in_dim(v, 0, by, axis=axis)]
    else:
        parts = [lax.slice_in_dim(v, n + by, n, axis=axis), lax.slice_in_dim(v, 0, n + by, axis=axis)]
    return jnp.concatenate(parts, axis=axis)


def window(v, core):
    n = v.shape[-2]
    first = jnp.concatenate([v[..., n - 4 :, :], v[..., :12, :]], axis=-2)
    return jnp.where(core == 0, first, v[..., 4:20, :])


def ring(n_x, core, mine, theirs, rows):
    parts = []
    for dx in range(n_x):
        a, b = (ref[first : first + 16, :].astype(F32).reshape(2, 8, 512) for ref, first in (rows(mine, dx), rows(theirs, dx)))
        parts += [jnp.where(core == 0, a, b), jnp.where(core == 0, b, a)]
    return jnp.concatenate(parts, axis=1)


def assemble(n_x, which, pieces, put):
    _, core, _, side = place()
    n = 2 * n_x
    for dy in range(2):
        slot = side if dy == 0 else 1 - side
        for pair in range(4):
            rows = lambda refs, dx: (refs[dx * 2 + dy], which * 64 + pair * 16)
            put(which, 2 + 8 * slot + 2 * pair, ring(n_x, core, pieces[:n], pieces[n:], rows))


def putter(vol, cot):
    def put(which, row, line):
        for s in range(3):
            (vol, cot)[which][s, pl.ds(row, 2)] = shifted(line, (s - 1, 1 - s)[which]).astype(BF16)

    return put


def both(w):
    return jnp.concatenate([w[CH:], w[: 2 * CH]], axis=1)


def place():
    gx, gy = lax.axis_index("gx"), lax.axis_index("gy")
    return gx, lax.rem(gx, 2), lax.div(gy, 2), lax.rem(gy, 2)


def edge_kernel(n_x, *refs):
    *pieces, last = refs
    side = place()[3]
    for dx in range(n_x):
        for which in range(2):
            a, b = pieces[dx * 2], pieces[dx * 2 + 1]
            out = slice(dx * 32 + which * 16, dx * 32 + which * 16 + 16)
            rows = slice(which * 64 + 48, which * 64 + 64)
            last[out, :] = jnp.where(side == 0, b[rows, :], a[rows, :])


def lines_kernel(fields, out, rows):
    sy, sx = rows.shape[:2]
    for k in range(2):
        for x in range(sx):
            block = fields[k, x].astype(F32)
            rows[:, x, :CH] = block[:, 0, :]
            rows[:, x, CH:] = block[:, 1, :]
        out[k * sy * sx : (k + 1) * sy * sx, :] = rows[...].reshape(sy * sx, 2 * CH).astype(BF16)


def later_kernel(lines, _, __, out):
    out[...] = lines[...]


def silu_t(pre):
    return (pre * jax.nn.sigmoid(pre)).T.astype(BF16)


def inner_kernel(n_x, *refs):
    *pieces, w_ref, outer, hid, vol, cot, pre = refs
    full = 16 * n_x
    put = putter(vol, cot)
    vol[:, :2] = jnp.zeros_like(vol[:, :2])
    assemble(n_x, 0, pieces, put)
    for k in range(9):
        left = vol[k // 3, k % 3 : k % 3 + 16].reshape(16 * full, 512)
        term = dot(left, both(w_ref[k * 768 : k * 768 + 768, :]))
        pre[...] = term if k == 0 else pre[...] + term
    outer[...] = pre[: 2 * full, :]
    hid[:, : 14 * full] = silu_t(pre[2 * full :, :])
    assemble(n_x, 1, pieces, put)


def gradient_kernel(n_x, n_z, groups, strip, block, scale, *refs):
    beyond_a, beyond_b, w_ref, outer, cot, hid_ref, near_vol, near_cot, own_out, *sends, ends, grad, flat = refs
    gx, core, z, side = place()
    full = 16 * n_x
    put = putter(near_vol, near_cot)
    for which in range(2):
        put(which, 0, ring(n_x, core, beyond_a, beyond_b, lambda ref, dx: (ref, dx * 32 + which * 16)))
    ends[:, :2] = near_cot[...]
    ends[:, 2:] = cot[:, 2:4]
    pre, first_line = outer[...], None
    for a in range(3):
        left = near_vol[a].reshape(2 * full, 512)
        w = w_ref[a * 2304 : a * 2304 + 1536, :]
        pre = pre + dot(left, both(w[:768]))
        term = dot(left[full:], both(w[768:]))
        first_line = term if a == 0 else first_line + term
    pre = jnp.concatenate([pre[:full] + first_line, pre[full:]], axis=0)
    hid = jnp.concatenate([hid_ref[:, : 14 * full], silu_t(pre)], axis=1)
    first = lax.div(gx * strip, 3 * CH)
    for k in range(groups):
        ab = jnp.minimum(first + k, 8)
        shift, row = lax.div(ab, 3), 2 - lax.rem(ab, 3)
        right = jnp.concatenate([cot[shift, pl.ds(row + 2, 14)], ends[shift, pl.ds(row, 2)]], axis=0).reshape(16 * full, 512)
        product = dot(hid, right) * scale
        at = k * 3 * CH
        grad[at : at + CH, :] = product[:CH, CH:]
        grad[at + CH : at + 2 * CH, :] = product[:CH, :CH] + product[CH:, CH:]
        grad[at + 2 * CH : at + 3 * CH, :] = product[CH:, :CH]

    for k in range(n_z):
        start = gx * strip + (2 * lax.rem(z + k, n_z) + side) * block - first * 3 * CH
        if block % 8 == 0:
            value = grad[pl.ds(pl.multiple_of(start, 8), block), :]
        else:
            over = lax.rem(start, 8)
            rows = (block + 7 + 7) // 8 * 8
            value = grad[pl.ds(pl.multiple_of(start - over, 8), rows), :]
            value = pltpu.roll(value, lax.rem(rows - over, rows), 0)[:block]
        for half in range(2):
            flat[pl.ds(half, block, stride=2), :] = value[:, half * 128 : half * 128 + 128]
        if k == 0:
            own_out[...] = flat[...]
        else:
            sends[k - 1][...] = flat[...].astype(BF16)


def first_kernel(n_x, *refs):
    *pieces, out = refs
    _, core, _, side = place()
    n = 2 * n_x
    for which in range(2):
        low, high = (
            ring(n_x, core, pieces[:n], pieces[n:], lambda refs, dx: (refs[dx * 2 + dy], which * 64)) for dy in range(2)
        )
        lines = window(jnp.where(side == 0, low, high), core)
        out[which * 32 : which * 32 + 32, :] = lines.reshape(32, 512).astype(BF16)


def local_kernel(vol_ref, cot_ref, near_vol, near_cot, after_ref, w1, w2, out_ref, vgrad_ref, vol, hid, cot, thr, acc):
    _, core, _, side = place()

    def cut(which, ref, near):
        before = jnp.where(side == 0, near[1].astype(F32), ref[1, 8:10].astype(F32))
        lines = [before, ref[1, pl.ds(2 + side * 8, 8)].astype(F32)]
        after = after_ref[which * 32 : which * 32 + 32, :].astype(F32).reshape(2, 16, 512)
        after = jnp.where(side == 0, window(ref[1, 10:12].astype(F32), core), after)
        return jnp.concatenate([window(jnp.concatenate(lines, axis=0), core), after], axis=0)

    v, c = cut(0, vol_ref, near_vol), cut(1, cot_ref, near_cot)
    for s in range(3):
        vol[s] = shifted(v, s - 1).astype(BF16)
        cot[s] = shifted(c, s - 1).astype(BF16)

    for k in range(9):
        left = vol[k // 3, k % 3 : k % 3 + 10].reshape(160, 512)
        term = dot(left, both(w1[k * 768 : k * 768 + 768, :]))
        acc[...] = term if k == 0 else acc[...] + term
    pre = acc[...].reshape(10, 16, 512)
    sig = jax.nn.sigmoid(pre)
    for s in range(3):
        hid[s] = shifted(pre * sig, s - 1).astype(BF16)
    slope = sig * (1.0 + pre * (1.0 - sig))

    for k in range(9):
        left = cot[k // 3, k % 3 : k % 3 + 10].reshape(160, 512)
        term = dot_t(left, both(w2[(8 - k) * 768 : (8 - k) * 768 + 768, :]))
        acc[...] = term if k == 0 else acc[...] + term
    through = acc[...].reshape(10, 16, 512) * slope
    for s in range(3):
        thr[s] = shifted(through, s - 1).astype(BF16)

    for k in range(9):
        left = hid[k // 3, k % 3 : k % 3 + 8].reshape(128, 512)
        term = dot(left, both(w2[k * 768 : k * 768 + 768, :]))
        acc[:128] = term if k == 0 else acc[:128] + term
    out_ref[...] = acc[:128].reshape(8, 16, 512)[:, 4:12].astype(BF16)

    for k in range(9):
        left = thr[k // 3, k % 3 : k % 3 + 8].reshape(128, 512)
        term = dot_t(left, both(w1[(8 - k) * 768 : (8 - k) * 768 + 768, :]))
        acc[:128] = term if k == 0 else acc[:128] + term
    vgrad_ref[...] = acc[:128].reshape(8, 16, 512)[:, 4:12].astype(BF16)


def params(mib):
    return pltpu.CompilerParams(vmem_limit_bytes=mib * 1024 * 1024)


def cost(us):
    return pl.CostEstimate(flops=us * 10**9, bytes_accessed=us * 3 * 10**6, transcendentals=0)


def body(volume, first_weight, second_weight, cotangent):
    sx, sy, sz, chans = volume.shape
    n_gx, n_gy = lax.axis_size("gx"), lax.axis_size("gy")
    n_x, n_z = n_gx // 2, n_gy // 2
    scale = 1.0 / float(sx * n_gx * sy * n_gy * sz) ** 0.5
    strip = ROWS // n_gx
    block = strip // n_gy
    groups = max(-(-(i + 1) * strip // (3 * CH)) - i * strip // (3 * CH) for i in range(n_gx))
    full = sx * n_gx
    perm = functools.partial(permutation, n_gx, n_gy)
    vmem = pl.BlockSpec(memory_space=pltpu.VMEM)

    def across(v):
        return lax.ppermute(v, AX, perm(lambda x, c, z, y: (x, 1 - c, z, y)))

    own = pl.pallas_call(
        lines_kernel,
        out_shape=jax.ShapeDtypeStruct((2 * sy * sx, sz * chans), BF16),
        in_specs=[vmem],
        out_specs=vmem,
        scratch_shapes=[pltpu.VMEM((sy, sx, sz * chans), F32)],
        compiler_params=params(4),
        cost_estimate=cost(1),
        name="lines",
    )(jnp.stack([volume, cotangent]))
    pieces = [own]
    for dx in range(n_x):
        for dy in range(2):
            if dx or dy:
                pieces.append(lax.ppermute(own, AX, perm(lambda x, c, z, y, dx=dx, dy=dy: (x - dx, c, z, y ^ dy))))
    last = pl.pallas_call(
        functools.partial(edge_kernel, n_x),
        out_shape=jax.ShapeDtypeStruct((n_x * 32, 512), BF16),
        in_specs=[vmem] * (2 * n_x),
        out_specs=vmem,
        compiler_params=params(4),
        cost_estimate=cost(4),
        name="edges",
    )(*pieces)
    pieces += [across(v) for v in pieces]
    beyond = lax.ppermute(last, AX, perm(lambda x, c, z, y: (x, c, z + 1, y)))

    first = pl.pallas_call(
        functools.partial(first_kernel, n_x),
        out_shape=jax.ShapeDtypeStruct((64, 512), BF16),
        in_specs=[vmem] * (4 * n_x),
        out_specs=vmem,
        compiler_params=params(4),
        cost_estimate=cost(0),
        name="first_lines",
    )(*pieces)
    after = lax.ppermute(first, AX, perm(lambda x, c, z, y: (x, c, z - 1, y)))

    plane = jax.ShapeDtypeStruct((3, 18, full, 512), BF16)
    columns = jax.ShapeDtypeStruct((512, 16 * full), BF16)
    outer, hid, vol, cot = pl.pallas_call(
        functools.partial(inner_kernel, n_x),
        out_shape=[jax.ShapeDtypeStruct((2 * full, 512), F32), columns, plane, plane],
        in_specs=[vmem] * (4 * n_x + 1),
        out_specs=[vmem] * 4,
        scratch_shapes=[pltpu.VMEM((16 * full, 512), F32)],
        compiler_params=params(24),
        cost_estimate=cost(5),
        name="plane_inner",
    )(*pieces, first_weight)
    beyond = pl.pallas_call(
        later_kernel,
        out_shape=jax.ShapeDtypeStruct(beyond.shape, BF16),
        in_specs=[vmem] * 3,
        out_specs=vmem,
        compiler_params=params(4),
        cost_estimate=cost(0),
        name="later",
    )(beyond, outer, first)
    near = jax.ShapeDtypeStruct((3, 2, full, 512), BF16)
    near_vol, near_cot, mine, *sends = pl.pallas_call(
        functools.partial(gradient_kernel, n_x, n_z, groups, strip, block, scale),
        out_shape=[near, near, jax.ShapeDtypeStruct((2 * block, 128), F32)]
        + [jax.ShapeDtypeStruct((2 * block, 128), BF16)] * (n_z - 1),
        in_specs=[vmem] * 6,
        out_specs=[vmem] * (2 + n_z),
        scratch_shapes=[
            pltpu.VMEM((3, 4, full, 512), BF16),
            pltpu.VMEM((groups * 3 * CH + (0 if block % 8 == 0 else 16), CH), F32),
            pltpu.VMEM((2 * block, 128), F32),
        ],
        compiler_params=params(24),
        cost_estimate=cost(0),
        name="plane_gradient",
    )(beyond, across(beyond), first_weight, outer, cot, hid)

    received = [
        lax.ppermute(sends[k - 1], AX, perm(lambda x, c, z, y, k=k: (x, c, z + k, y)))
        for k in sorted(range(n_z - 1, 0, -1), key=lambda k: k != n_z // 2)
    ]

    output, volume_grad = pl.pallas_call(
        local_kernel,
        out_shape=[jax.ShapeDtypeStruct((sy, sx, 512), BF16)] * 2,
        in_specs=[vmem] * 7,
        out_specs=[vmem] * 2,
        scratch_shapes=[
            pltpu.VMEM((3, 12, 16, 512), BF16),
            pltpu.VMEM((3, 10, 16, 512), BF16),
            pltpu.VMEM((3, 12, 16, 512), BF16),
            pltpu.VMEM((3, 10, 16, 512), BF16),
            pltpu.VMEM((160, 512), F32),
        ],
        compiler_params=params(24),
        cost_estimate=cost(0),
        name="local_convolutions",
    )(vol, cot, near_vol, near_cot, after, first_weight, second_weight)

    def cells(v):
        return jnp.transpose(v.reshape(sy, sx, sz, chans), (1, 0, 2, 3))

    total = mine
    for v in received:
        total = total + v.astype(F32)
    return cells(output), cells(volume_grad), total.reshape(-1)


def solution(mesh):
    in_specs = (P("gx", "gy", None, None), P(), P(), P("gx", "gy", None, None))
    out_specs = (P("gx", "gy", None, None), P("gx", "gy", None, None), P(("gx", "gy")))
    return jax.shard_map(body, mesh=mesh, in_specs=in_specs, out_specs=out_specs, check_vma=False)
```

```python
import functools

import jax
import jax.numpy as jnp
from jax import lax
from jax.experimental import pallas as pl
from jax.experimental.pallas import tpu as pltpu
from jax.sharding import PartitionSpec as P

AX = ("gx", "gy")
F32 = jnp.float32
BF16 = jnp.bfloat16
CH = 256
ROWS = 27 * CH


def permutation(n_gx, n_gy, move):
    pairs = []
    for i in range(n_gx):
        for j in range(n_gy):
            x, c, z, y = move(i // 2, i % 2, j // 2, j % 2)
            x, z = x % (n_gx // 2), z % (n_gy // 2)
            pairs.append((i * n_gy + j, (x * 2 + c) * n_gy + z * 2 + y))
    return pairs


def dot(a, b):
    return lax.dot_general(a, b, (((1,), (0,)), ((), ())), preferred_element_type=F32)


def dot_t(a, b):
    return lax.dot_general(a, b, (((1,), (1,)), ((), ())), preferred_element_type=F32)


def shifted(v, by):
    if by == 0:
        return v
    axis, n = v.ndim - 2, v.shape[-2]
    if by > 0:
        parts = [lax.slice_in_dim(v, by, n, axis=axis), lax.slice_in_dim(v, 0, by, axis=axis)]
    else:
        parts = [lax.slice_in_dim(v, n + by, n, axis=axis), lax.slice_in_dim(v, 0, n + by, axis=axis)]
    return jnp.concatenate(parts, axis=axis)


def window(v, core):
    n = v.shape[-2]
    first = jnp.concatenate([v[..., n - 4 :, :], v[..., :12, :]], axis=-2)
    return jnp.where(core == 0, first, v[..., 4:20, :])


def ring(n_x, core, mine, theirs, rows):
    parts = []
    for dx in range(n_x):
        a, b = (ref[first : first + 16, :].astype(F32).reshape(2, 8, 512) for ref, first in (rows(mine, dx), rows(theirs, dx)))
        parts += [jnp.where(core == 0, a, b), jnp.where(core == 0, b, a)]
    return jnp.concatenate(parts, axis=1)


def assemble(n_x, which, pieces, put):
    _, core, _, side = place()
    n = 2 * n_x
    for dy in range(2):
        slot = side if dy == 0 else 1 - side
        for pair in range(4):
            rows = lambda refs, dx: (refs[dx * 2 + dy], which * 64 + pair * 16)
            put(which, 2 + 8 * slot + 2 * pair, ring(n_x, core, pieces[:n], pieces[n:], rows))


def putter(vol, cot):
    def put(which, row, line):
        for s in range(3):
            (vol, cot)[which][s, pl.ds(row, 2)] = shifted(line, (s - 1, 1 - s)[which]).astype(BF16)

    return put


def both(w):
    return jnp.concatenate([w[CH:], w[: 2 * CH]], axis=1)


def place():
    gx, gy = lax.axis_index("gx"), lax.axis_index("gy")
    return gx, lax.rem(gx, 2), lax.div(gy, 2), lax.rem(gy, 2)


def edge_kernel(n_x, *refs):
    *pieces, last = refs
    side = place()[3]
    for dx in range(n_x):
        for which in range(2):
            a, b = pieces[dx * 2], pieces[dx * 2 + 1]
            out = slice(dx * 32 + which * 16, dx * 32 + which * 16 + 16)
            rows = slice(which * 64 + 48, which * 64 + 64)
            last[out, :] = jnp.where(side == 0, b[rows, :], a[rows, :])


def lines_kernel(fields, out, rows):
    sy, sx = rows.shape[:2]
    for k in range(2):
        for x in range(sx):
            block = fields[k, x].astype(F32)
            rows[:, x, :CH] = block[:, 0, :]
            rows[:, x, CH:] = block[:, 1, :]
        out[k * sy * sx : (k + 1) * sy * sx, :] = rows[...].reshape(sy * sx, 2 * CH).astype(BF16)


def later_kernel(lines, _, __, out):
    out[...] = lines[...]


def silu_t(pre):
    return (pre * jax.nn.sigmoid(pre)).T.astype(BF16)


def inner_kernel(n_x, *refs):
    *pieces, w_ref, outer, hid, vol, cot, pre = refs
    full = 16 * n_x
    put = putter(vol, cot)
    vol[:, :2] = jnp.zeros_like(vol[:, :2])
    assemble(n_x, 0, pieces, put)
    for k in range(9):
        left = vol[k // 3, k % 3 : k % 3 + 16].reshape(16 * full, 512)
        term = dot(left, both(w_ref[k * 768 : k * 768 + 768, :]))
        pre[...] = term if k == 0 else pre[...] + term
    outer[...] = pre[: 2 * full, :]
    hid[:, : 14 * full] = silu_t(pre[2 * full :, :])
    assemble(n_x, 1, pieces, put)


def gradient_kernel(n_x, n_z, groups, strip, block, scale, *refs):
    beyond_a, beyond_b, w_ref, outer, cot, hid_ref, near_vol, near_cot, own_out, *sends, ends, grad = refs
    gx, core, z, side = place()
    full = 16 * n_x
    put = putter(near_vol, near_cot)
    for which in range(2):
        put(which, 0, ring(n_x, core, beyond_a, beyond_b, lambda ref, dx: (ref, dx * 32 + which * 16)))
    ends[:, :2] = near_cot[...]
    ends[:, 2:] = cot[:, 2:4]
    pre, first_line = outer[...], None
    for a in range(3):
        left = near_vol[a].reshape(2 * full, 512)
        w = w_ref[a * 2304 : a * 2304 + 1536, :]
        pre = pre + dot(left, both(w[:768]))
        term = dot(left[full:], both(w[768:]))
        first_line = term if a == 0 else first_line + term
    pre = jnp.concatenate([pre[:full] + first_line, pre[full:]], axis=0)
    hid = jnp.concatenate([hid_ref[:, : 14 * full], silu_t(pre)], axis=1)
    first = lax.div(gx * strip, 3 * CH)
    for k in range(groups):
        ab = jnp.minimum(first + k, 8)
        shift, row = lax.div(ab, 3), 2 - lax.rem(ab, 3)
        right = jnp.concatenate([cot[shift, pl.ds(row + 2, 14)], ends[shift, pl.ds(row, 2)]], axis=0).reshape(16 * full, 512)
        product = dot(hid, right) * scale
        terms = (product[:CH, CH:], product[:CH, :CH] + product[CH:, CH:], product[CH:, :CH])
        for e, term in enumerate(terms):
            for half in range(2):
                grad[pl.ds((k * 3 + e) * 2 * CH + half, CH, stride=2), :] = term[:, half * 128 : half * 128 + 128]

    size = 2 * block
    for k in range(n_z):
        start = 2 * (gx * strip + (2 * lax.rem(z + k, n_z) + side) * block - first * 3 * CH)
        if size % 8 == 0:
            value = grad[pl.ds(pl.multiple_of(start, 8), size), :]
        else:
            over = lax.rem(start, 8)
            rows = (size + 7 + 7) // 8 * 8
            value = grad[pl.ds(pl.multiple_of(start - over, 8), rows), :]
            value = pltpu.roll(value, lax.rem(rows - over, rows), 0)[:size]
        if k == 0:
            own_out[...] = value
        else:
            sends[k - 1][...] = value.astype(BF16)


def first_kernel(n_x, *refs):
    *pieces, out = refs
    _, core, _, side = place()
    n = 2 * n_x
    for which in range(2):
        low, high = (
            ring(n_x, core, pieces[:n], pieces[n:], lambda refs, dx: (refs[dx * 2 + dy], which * 64)) for dy in range(2)
        )
        lines = window(jnp.where(side == 0, low, high), core)
        out[which * 32 : which * 32 + 32, :] = lines.reshape(32, 512).astype(BF16)


def local_kernel(vol_ref, cot_ref, near_vol, near_cot, after_ref, w1, w2, out_ref, vgrad_ref, vol, hid, cot, thr, acc):
    _, core, _, side = place()

    def cut(which, ref, near):
        before = jnp.where(side == 0, near[1].astype(F32), ref[1, 8:10].astype(F32))
        lines = [before, ref[1, pl.ds(2 + side * 8, 8)].astype(F32)]
        after = after_ref[which * 32 : which * 32 + 32, :].astype(F32).reshape(2, 16, 512)
        after = jnp.where(side == 0, window(ref[1, 10:12].astype(F32), core), after)
        return jnp.concatenate([window(jnp.concatenate(lines, axis=0), core), after], axis=0)

    v, c = cut(0, vol_ref, near_vol), cut(1, cot_ref, near_cot)
    for s in range(3):
        vol[s] = shifted(v, s - 1).astype(BF16)
        cot[s] = shifted(c, s - 1).astype(BF16)

    for k in range(9):
        left = vol[k // 3, k % 3 : k % 3 + 10].reshape(160, 512)
        term = dot(left, both(w1[k * 768 : k * 768 + 768, :]))
        acc[...] = term if k == 0 else acc[...] + term
    pre = acc[...].reshape(10, 16, 512)
    sig = jax.nn.sigmoid(pre)
    for s in range(3):
        hid[s] = shifted(pre * sig, s - 1).astype(BF16)
    slope = sig * (1.0 + pre * (1.0 - sig))

    for k in range(9):
        left = cot[k // 3, k % 3 : k % 3 + 10].reshape(160, 512)
        term = dot_t(left, both(w2[(8 - k) * 768 : (8 - k) * 768 + 768, :]))
        acc[...] = term if k == 0 else acc[...] + term
    through = acc[...].reshape(10, 16, 512) * slope
    for s in range(3):
        thr[s] = shifted(through, s - 1).astype(BF16)

    for k in range(9):
        left = hid[k // 3, k % 3 : k % 3 + 8].reshape(128, 512)
        term = dot(left, both(w2[k * 768 : k * 768 + 768, :]))
        acc[:128] = term if k == 0 else acc[:128] + term
    out_ref[...] = acc[:128].reshape(8, 16, 512)[:, 4:12].astype(BF16)

    for k in range(9):
        left = thr[k // 3, k % 3 : k % 3 + 8].reshape(128, 512)
        term = dot_t(left, both(w1[(8 - k) * 768 : (8 - k) * 768 + 768, :]))
        acc[:128] = term if k == 0 else acc[:128] + term
    vgrad_ref[...] = acc[:128].reshape(8, 16, 512)[:, 4:12].astype(BF16)


def params(mib):
    return pltpu.CompilerParams(vmem_limit_bytes=mib * 1024 * 1024)


def cost(us):
    return pl.CostEstimate(flops=us * 10**9, bytes_accessed=us * 3 * 10**6, transcendentals=0)


def body(volume, first_weight, second_weight, cotangent):
    sx, sy, sz, chans = volume.shape
    n_gx, n_gy = lax.axis_size("gx"), lax.axis_size("gy")
    n_x, n_z = n_gx // 2, n_gy // 2
    scale = 1.0 / float(sx * n_gx * sy * n_gy * sz) ** 0.5
    strip = ROWS // n_gx
    block = strip // n_gy
    groups = max(-(-(i + 1) * strip // (3 * CH)) - i * strip // (3 * CH) for i in range(n_gx))
    full = sx * n_gx
    perm = functools.partial(permutation, n_gx, n_gy)
    vmem = pl.BlockSpec(memory_space=pltpu.VMEM)

    def across(v):
        return lax.ppermute(v, AX, perm(lambda x, c, z, y: (x, 1 - c, z, y)))

    own = pl.pallas_call(
        lines_kernel,
        out_shape=jax.ShapeDtypeStruct((2 * sy * sx, sz * chans), BF16),
        in_specs=[vmem],
        out_specs=vmem,
        scratch_shapes=[pltpu.VMEM((sy, sx, sz * chans), F32)],
        compiler_params=params(4),
        cost_estimate=cost(1),
        name="lines",
    )(jnp.stack([volume, cotangent]))
    pieces = [own]
    for dx in range(n_x):
        for dy in range(2):
            if dx or dy:
                pieces.append(lax.ppermute(own, AX, perm(lambda x, c, z, y, dx=dx, dy=dy: (x - dx, c, z, y ^ dy))))
    last = pl.pallas_call(
        functools.partial(edge_kernel, n_x),
        out_shape=jax.ShapeDtypeStruct((n_x * 32, 512), BF16),
        in_specs=[vmem] * (2 * n_x),
        out_specs=vmem,
        compiler_params=params(4),
        cost_estimate=cost(4),
        name="edges",
    )(*pieces)
    pieces += [across(v) for v in pieces]
    beyond = lax.ppermute(last, AX, perm(lambda x, c, z, y: (x, c, z + 1, y)))

    first = pl.pallas_call(
        functools.partial(first_kernel, n_x),
        out_shape=jax.ShapeDtypeStruct((64, 512), BF16),
        in_specs=[vmem] * (4 * n_x),
        out_specs=vmem,
        compiler_params=params(4),
        cost_estimate=cost(0),
        name="first_lines",
    )(*pieces)
    after = lax.ppermute(first, AX, perm(lambda x, c, z, y: (x, c, z - 1, y)))

    plane = jax.ShapeDtypeStruct((3, 18, full, 512), BF16)
    columns = jax.ShapeDtypeStruct((512, 16 * full), BF16)
    outer, hid, vol, cot = pl.pallas_call(
        functools.partial(inner_kernel, n_x),
        out_shape=[jax.ShapeDtypeStruct((2 * full, 512), F32), columns, plane, plane],
        in_specs=[vmem] * (4 * n_x + 1),
        out_specs=[vmem] * 4,
        scratch_shapes=[pltpu.VMEM((16 * full, 512), F32)],
        compiler_params=params(24),
        cost_estimate=cost(5),
        name="plane_inner",
    )(*pieces, first_weight)
    beyond = pl.pallas_call(
        later_kernel,
        out_shape=jax.ShapeDtypeStruct(beyond.shape, BF16),
        in_specs=[vmem] * 3,
        out_specs=vmem,
        compiler_params=params(4),
        cost_estimate=cost(0),
        name="later",
    )(beyond, outer, first)
    near = jax.ShapeDtypeStruct((3, 2, full, 512), BF16)
    near_vol, near_cot, mine, *sends = pl.pallas_call(
        functools.partial(gradient_kernel, n_x, n_z, groups, strip, block, scale),
        out_shape=[near, near, jax.ShapeDtypeStruct((2 * block, 128), F32)]
        + [jax.ShapeDtypeStruct((2 * block, 128), BF16)] * (n_z - 1),
        in_specs=[vmem] * 6,
        out_specs=[vmem] * (2 + n_z),
        scratch_shapes=[
            pltpu.VMEM((3, 4, full, 512), BF16),
            pltpu.VMEM((groups * 6 * CH + (0 if 2 * block % 8 == 0 else 16), 128), F32),
        ],
        compiler_params=params(24),
        cost_estimate=cost(0),
        name="plane_gradient",
    )(beyond, across(beyond), first_weight, outer, cot, hid)

    received = [
        lax.ppermute(sends[k - 1], AX, perm(lambda x, c, z, y, k=k: (x, c, z + k, y)))
        for k in sorted(range(n_z - 1, 0, -1), key=lambda k: k != n_z // 2)
    ]

    output, volume_grad = pl.pallas_call(
        local_kernel,
        out_shape=[jax.ShapeDtypeStruct((sy, sx, 512), BF16)] * 2,
        in_specs=[vmem] * 7,
        out_specs=[vmem] * 2,
        scratch_shapes=[
            pltpu.VMEM((3, 12, 16, 512), BF16),
            pltpu.VMEM((3, 10, 16, 512), BF16),
            pltpu.VMEM((3, 12, 16, 512), BF16),
            pltpu.VMEM((3, 10, 16, 512), BF16),
            pltpu.VMEM((160, 512), F32),
        ],
        compiler_params=params(24),
        cost_estimate=cost(0),
        name="local_convolutions",
    )(vol, cot, near_vol, near_cot, after, first_weight, second_weight)

    def cells(v):
        return jnp.transpose(v.reshape(sy, sx, sz, chans), (1, 0, 2, 3))

    total = mine
    for v in received:
        total = total + v.astype(F32)
    return cells(output), cells(volume_grad), total.reshape(-1)


def solution(mesh):
    in_specs = (P("gx", "gy", None, None), P(), P(), P("gx", "gy", None, None))
    out_specs = (P("gx", "gy", None, None), P("gx", "gy", None, None), P(("gx", "gy")))
    return jax.shard_map(body, mesh=mesh, in_specs=in_specs, out_specs=out_specs, check_vma=False)
```
